512 devices in a mesh: group: 64 (over x, z_lo, core), tensor: 8 (over y, z_hi).
Axes of the slice: x: 4, y: 4, z: 16 (z_hi: 2, z_lo: 8; z = z_hi * 8 + z_lo), core: 2. Of those that a mesh axis runs over, the one named last changes fastest.
Arguments:
- cache_blocks: bfloat16 [4096, 1, 128, 8, 256], P('group', None, 'tensor'), may hold values from -6 to 6
- prompt_len: int32 [64, 64], replicated, may hold values from 1 to 128, 2730 in all within a row
- dest_perm: int32 [64, 64], replicated, may hold values from 0 to 63, each once within a row
- new_q: bfloat16 [64, 64, 4, 64, 128], P('group', None, None, 'tensor'), may hold values from -170 to 170
- new_kv: bfloat16 [64, 64, 4, 8, 256], P('group', None, None, 'tensor'), may hold values from -6 to 6
Outputs:
- attended: bfloat16 [64, 64, 4, 64, 128], P('group', None, None, 'tensor')
The draws below stay inside these ranges and needn't reach their ends.
Inputs may be any that keep to these rules, and one draw needn't show every extreme that they name: Prompt j of group s goes to decode group dest_perm[s, j]; each row of dest_perm names every decode group once, so every decode group receives exactly one prompt from each holding group. `prompt_len`: the lengths of one group's prompts sum to 2730, and one of them is 128.
All inputs are finite; a program needn't handle non-finite values.
Results may differ from the reference program's by a relative error of at most 0.0049.
Values may be sent and summed in bfloat16 or wider, within the bound.
A program may use at most 64 MiB of HBM per device.

```python
import math
import jax
import jax.numpy as jnp
import numpy as np
from jax import lax

HD = 128
KVH = 8
QH = 64
BLK = 128
MAXB = 1
STEPS = 4
REQ = 64
REQS = 4096
N_GROUP = 64


def key_part(key):
    shape = (N_GROUP, N_GROUP, STEPS, KVH, HD)
    common = jax.random.normal(jax.random.fold_in(key, 101), shape, jnp.float32)
    return jnp.clip(common, -6.0, 6.0)


def draw_new_kv(key, part):
    fresh_keys = key_part(key)
    key = jax.random.fold_in(key, 3)
    values = jnp.clip(jax.random.normal(key, (N_GROUP, N_GROUP, STEPS, KVH, HD), jnp.float32), -6.0, 6.0)
    return jnp.concatenate([fresh_keys, values], axis=-1).astype(jnp.bfloat16)


def draw_new_q(key, part):
    key = jax.random.fold_in(key, 5)
    shape = (N_GROUP, N_GROUP, STEPS, QH, HD)
    noise = jnp.clip(jax.random.normal(jax.random.fold_in(key, 1), shape, jnp.float32), -6.0, 6.0)
    queries = noise
    return queries.astype(jnp.bfloat16)


def block_levels(stream_key, dims, split, least, largest):
    gain = 1.0
    for axis_at, parts in split:
        draws = jax.random.uniform(jax.random.fold_in(jax.random.fold_in(stream_key, 6), axis_at), (parts,), jnp.float32, least / len(split), largest / len(split))
        gain = gain * jnp.repeat(jnp.exp(draws), dims[axis_at] // parts).reshape((-1,) + (1,) * (len(dims) - 1 - axis_at))
    return gain


def profile(count, total, bound, lean):
    portions = [(1 << 20) // math.isqrt(grade ** lean) + 1 for grade in range(2, count + 1)]
    spare, counts = total - bound - (count - 1), [1] * (count - 1)
    while spare > 0:
        candidates = [i for i in range(count - 1) if counts[i] < bound]
        pool, remaining = sum([portions[i] for i in candidates]), spare
        for i in candidates:
            extra = min(bound - counts[i], max(1, remaining * portions[i] // pool), spare)
            counts[i] = counts[i] + extra
            spare = spare - extra
    return np.array([bound] + counts)


def ragged(key, amount, total, reach, slope):
    if amount == 2:
        one = jax.random.randint(key, (), max(1, total - reach), min(reach, total - 1) + 1)
        return jnp.stack([one, total - one])
    tallies = jnp.asarray(profile(amount, total, reach, slope), jnp.int32)
    twos = (amount - 1) // 2
    donor, sink = tallies[1:1 + 2 * twos:2], tallies[2:2 + 2 * twos:2]
    slack = jnp.minimum(donor - 1, reach - sink)
    shifted = jax.random.randint(jax.random.fold_in(key, 1), (twos,), 0, 1 << 20) % (slack + 1)
    tallies = tallies.at[1:1 + 2 * twos:2].set(donor - shifted).at[2:2 + 2 * twos:2].set(sink + shifted)
    return tallies[jax.random.permutation(jax.random.fold_in(key, 2), amount)]


def normal_values(rng, extent, scale, reach, shards=(), kind=jnp.bfloat16):
    level = block_levels(rng, extent, shards, -0.22, 0.18) if shards else 1.0
    entries = jax.random.normal(rng, extent, jnp.float32) * scale * level
    return jnp.minimum(jnp.maximum(entries, -reach), reach).astype(kind)


def setup_inputs(seed: int = 0) -> dict:
    seeds = jax.random.split(jax.random.key(seed), 6)
    return {
        "cache_blocks": normal_values(seeds[0], (REQS, MAXB, BLK, KVH, 2 * HD), 1.0, 6.0, ((0, 64), (2, 8))),
        "prompt_len": jax.vmap(lambda own: ragged(own, REQ, REQ * MAXB * BLK // 3, MAXB * BLK, 2))(jax.random.split(seeds[1], N_GROUP)).reshape((N_GROUP, REQ)).astype(jnp.int32),
        "dest_perm": jax.vmap(lambda own: jax.random.permutation(own, N_GROUP))(jax.random.split(seeds[2], N_GROUP)).reshape((N_GROUP, N_GROUP)).astype(jnp.int32),
        "new_q": draw_new_q(jax.random.fold_in(seeds[5], 71), 0),
        "new_kv": draw_new_kv(jax.random.fold_in(seeds[5], 71), 0),
    }


def reference(cache_blocks, prompt_len, dest_perm, new_q, new_kv):
    group_ids = jnp.arange(N_GROUP, dtype=jnp.int32)
    score_scale = 1.0 / math.sqrt(HD)
    share = QH // KVH

    def one_group(own_group):
        matches = dest_perm == own_group
        position = lax.optimization_barrier(jnp.sum(jnp.where(matches, group_ids[None, :], 0), axis=1)).astype(jnp.int32)
        is_live = position < REQ
        chosen_req = jnp.minimum(position, REQ - 1).astype(jnp.int32)
        context_len = jnp.where(is_live, jnp.take_along_axis(prompt_len, chosen_req[:, None], axis=1)[:, 0], 0)
        source_rows = (group_ids * REQ + chosen_req).astype(jnp.int32)
        context = jnp.take(cache_blocks, source_rows, axis=0).reshape(N_GROUP, MAXB * BLK, KVH, 2 * HD)
        context = context.astype(jnp.float32)
        ctx_keys = context[..., :HD]
        ctx_vals = context[..., HD:]
        queries = lax.dynamic_index_in_dim(new_q, own_group, 0, keepdims=False).astype(jnp.float32)
        queries = queries.reshape(N_GROUP, STEPS, KVH, share, HD)
        fresh = lax.dynamic_index_in_dim(new_kv, own_group, 0, keepdims=False).astype(jnp.float32)
        fresh_keys = fresh[..., :HD]
        fresh_vals = fresh[..., HD:]
        ctx_scores = jnp.einsum('stkgd,spkd->stkgp', queries, ctx_keys) * score_scale
        new_scores = jnp.einsum('stkgd,sukd->stkgu', queries, fresh_keys) * score_scale
        token_pos = jnp.arange(MAXB * BLK, dtype=jnp.int32)
        ctx_mask = token_pos[None, :] < context_len[:, None]
        ctx_scores = jnp.where(ctx_mask[:, None, None, None, :], ctx_scores, -1e+30)
        step_ids = jnp.arange(STEPS, dtype=jnp.int32)
        causal = step_ids[None, :] <= step_ids[:, None]
        new_scores = jnp.where(causal[None, :, None, None, :], new_scores, -1e+30)
        row_max = jnp.maximum(lax.optimization_barrier(jnp.max(ctx_scores, axis=-1)), lax.optimization_barrier(jnp.max(new_scores, axis=-1)))
        ctx_expo = jnp.exp(ctx_scores - row_max[..., None])
        new_expo = jnp.exp(new_scores - row_max[..., None])
        denominator = lax.optimization_barrier(jnp.sum(ctx_expo, axis=-1)) + lax.optimization_barrier(jnp.sum(new_expo, axis=-1))
        ctx_probs = (ctx_expo / denominator[..., None]).astype(jnp.bfloat16).astype(jnp.float32)
        new_probs = (new_expo / denominator[..., None]).astype(jnp.bfloat16).astype(jnp.float32)
        result = jnp.einsum('stkgp,spkd->stkgd', ctx_probs, ctx_vals) + jnp.einsum('stkgu,sukd->stkgd', new_probs, fresh_vals)
        return result.reshape(N_GROUP, STEPS, QH, HD).astype(jnp.bfloat16)
    return lax.map(one_group, group_ids)
```

```python
import functools
import math

import jax
import jax.numpy as jnp
from jax import lax
from jax.experimental import pallas as pl
from jax.experimental.pallas import tpu as pltpu
from jax.sharding import PartitionSpec as P

MESH = pl.DeviceIdType.MESH

X, ZL, CORES = 4, 8, 2
ZH = 2
CHUNKS = 8
NONE = -1e30


def kernel(groups, tensors, cache_ref, pos_ref, len_ref, q_ref, fresh_ref, out_ref,
           cbuf, kvsend, kvrecv, qbuf, osend, orecv, ssend, srecv, fo, fm, fl,
           cache_sem, kv_send_sem, kv_recv_sem, q_send_sem, q_recv_sem,
           o_send_sem, o_recv_sem, s_send_sem, s_recv_sem):
    ys = tensors // ZH
    g = lax.axis_index("group")
    t = lax.axis_index("tensor")
    y, zh = t // ZH, t % ZH
    core, zl, x = g % CORES, (g // CORES) % ZL, g // (CORES * ZL)
    z = zh * ZL + zl
    rows = q_ref.shape[0]
    qn = q_ref.shape[1]
    head = q_ref.shape[2]
    tok = cache_ref.shape[1] // tensors
    piece = ZH * tok
    per = rows // CHUNKS
    scale = 1.0 / math.sqrt(head)
    inner = X * CORES

    def offsets(i):
        k, j = i // inner, inner - 1 - i % inner
        far = ZL // 2 + (k // 2) * (1 - k % 2) - ((k + 1) // 2) * (k % 2)
        return j // CORES, far, j % CORES

    def towards(i):
        dx, dz, dc = offsets(i)
        peer = (((x + dx) % X) * ZL + (zl + dz) % ZL) * CORES + (core + dc) % CORES
        return peer

    def source(i):
        dx, dz, dc = offsets(i)
        return (((x + X - dx) % X) * ZL + (zl + ZL - dz) % ZL) * CORES + (core + CORES - dc) % CORES

    last = groups - 1

    def cache_copy(c):
        return pltpu.make_async_copy(
            cache_ref.at[pl.ds(c * per, per)], cbuf.at[pl.ds(c * per, per)], cache_sem.at[c])

    for c in range(CHUNKS):
        cache_copy(c).start()

    barrier = pltpu.get_barrier_semaphore()

    def greet(i, _):
        peer = towards(i)
        for h in range(ZH):
            pl.semaphore_signal(barrier, inc=1, device_id=(peer, y * ZH + h), device_id_type=MESH)
        return 0

    lax.fori_loop(0, last, greet, 0)
    pl.semaphore_signal(barrier, inc=1, device_id=(g, y * ZH + 1 - zh), device_id_type=MESH)
    for k in range(1, ys):
        pl.semaphore_signal(barrier, inc=1, device_id=(g, ((y + k) % ys) * ZH + zh), device_id_type=MESH)
    pl.semaphore_wait(barrier, groups * ZH - 1 + ys - 1)

    def q_copy(peer, h):
        return pltpu.make_async_remote_copy(
            src_ref=q_ref.at[peer], dst_ref=qbuf.at[g, zh], send_sem=q_send_sem,
            recv_sem=q_recv_sem.at[g], device_id=(peer, y * ZH + h), device_id_type=MESH)

    def send_q(i, _):
        peer = towards(i)
        for h in range(ZH):
            q_copy(peer, h).start()
        return 0

    lax.fori_loop(0, last, send_q, 0)
    q_copy(g, 1 - zh).start()
    pltpu.make_async_copy(q_ref.at[g], qbuf.at[g, zh], q_recv_sem.at[g]).start()

    size = tensors * tok
    r_out = lax.broadcasted_iota(jnp.int32, (size, size), 0)
    r_in = lax.broadcasted_iota(jnp.int32, (size, size), 1)
    pair = r_out // piece + y
    pair = jnp.where(pair >= ys, pair - ys, pair)
    wanted = (r_out % tok) * tensors + pair * ZH + (r_out % piece) // tok
    shuffle = jnp.where(wanted == r_in, 1.0, 0.0).astype(jnp.bfloat16)

    def kv_copy(k, c):
        return pltpu.make_async_remote_copy(
            src_ref=kvsend.at[k - 1, pl.ds(c * per, per)],
            dst_ref=kvrecv.at[pl.ds(c * per, per), y],
            send_sem=kv_send_sem.at[k - 1, c], recv_sem=kv_recv_sem.at[k - 1, c],
            device_id=(g, ((y + k) % ys) * ZH + zh), device_id_type=MESH)

    for c in range(CHUNKS):
        cache_copy(c).wait()

        def regroup(i, _, c=c):
            r = c * per + i
            moved = jnp.dot(shuffle, cbuf[r], preferred_element_type=jnp.float32).astype(jnp.bfloat16)
            kvrecv[r, y] = moved[:piece]
            for k in range(1, ys):
                kvsend[k - 1, r] = moved[k * piece:(k + 1) * piece]
            return 0

        lax.fori_loop(0, per, regroup, 0)
        for k in range(1, ys):
            kv_copy(k, c).start()

    batch, fresh_rows = fresh_ref.shape[0], fresh_ref.shape[1]
    at = rows // batch
    steps = fresh_rows // at
    shape = (at * qn, fresh_rows)
    f_row = lax.broadcasted_iota(jnp.int32, shape, 0)
    f_col = lax.broadcasted_iota(jnp.int32, shape, 1)
    f_keep = ((f_row // qn) == (f_col // steps)) & ((f_col % steps) <= (f_row % qn) // (qn // steps))

    def fresh_part(b, _):
        q = q_ref[pl.ds(b * at, at)].reshape(at * qn, head)
        kv = fresh_ref[b]
        s = lax.dot_general(q, kv[:, :head], (((1,), (1,)), ((), ())), preferred_element_type=jnp.float32) * scale
        s = jnp.where(f_keep, s, NONE)
        m = jnp.max(s, axis=1, keepdims=True)
        p = jnp.exp(s - m)
        l = jnp.sum(p, axis=1, keepdims=True)
        o = jnp.dot(p.astype(jnp.bfloat16), kv[:, head:], preferred_element_type=jnp.float32)
        fo[pl.ds(b * at, at)] = o.reshape(at, qn, head)
        fm[pl.ds(b * at, at)] = jnp.broadcast_to(m, (at * qn, head)).reshape(at, qn, head)
        fl[pl.ds(b * at, at)] = jnp.broadcast_to(l, (at * qn, head)).reshape(at, qn, head)
        return 0

    lax.fori_loop(0, batch, fresh_part, 0)

    for c in range(CHUNKS):
        for k in range(1, ys):
            kv_copy(k, c).wait_recv()

    both = ZH * qn
    shape = (both, ys * piece)
    a_row = lax.broadcasted_iota(jnp.int32, shape, 0)
    a_col = lax.broadcasted_iota(jnp.int32, shape, 1)
    token = ((a_col // piece) * ZH + zh) * tok + a_col % tok
    token = jnp.where((a_col % piece) // tok == a_row // qn, token, 1 << 20)
    lane = lax.broadcasted_iota(jnp.int32, (both, head), 1)
    diag = lax.broadcasted_iota(jnp.int32, (both, head), 0) % qn
    on_m, on_l = lane == diag, lane == diag + qn

    def o_copy(peer, h):
        return pltpu.make_async_remote_copy(
            src_ref=osend.at[peer, h], dst_ref=orecv.at[g, zh], send_sem=o_send_sem,
            recv_sem=o_recv_sem.at[g], device_id=(peer, y * ZH + h), device_id_type=MESH)

    def s_copy(peer, h):
        return pltpu.make_async_remote_copy(
            src_ref=ssend.at[peer, h], dst_ref=srecv.at[g, zh], send_sem=s_send_sem,
            recv_sem=s_recv_sem.at[g], device_id=(peer, y * ZH + h), device_id_type=MESH)

    def attend(i):
        src = source(i)
        pltpu.make_async_copy(qbuf.at[src], qbuf.at[src], q_recv_sem.at[src]).wait()
        q = qbuf[src].reshape(both, head)
        kv = kvrecv[pos_ref[src]].reshape(ys * piece, 2 * head)
        s = lax.dot_general(q, kv[:, :head], (((1,), (1,)), ((), ())), preferred_element_type=jnp.float32) * scale
        keep = token < len_ref[src]
        s = jnp.where(keep, s, NONE)
        m = jnp.max(s, axis=1, keepdims=True)
        p = jnp.where(keep, jnp.exp(s - m), 0.0)
        l = jnp.sum(p, axis=1, keepdims=True)
        o = jnp.dot(p.astype(jnp.bfloat16), kv[:, head:], preferred_element_type=jnp.float32)
        osend[src] = o.astype(jnp.bfloat16).reshape(ZH, qn, head)
        stat = jnp.where(on_m, m, jnp.where(on_l, l, 0.0))
        ssend[src] = jnp.sum(stat.reshape(ZH, qn, head), axis=1, keepdims=True)
        return src

    def attend_send(i, _):
        src = attend(i)
        for h in range(ZH):
            o_copy(src, h).start()
            s_copy(src, h).start()
        return 0

    lax.fori_loop(0, last, attend_send, 0)
    attend(last)
    o_copy(g, 1 - zh).start()
    s_copy(g, 1 - zh).start()
    pltpu.make_async_copy(osend.at[g, zh], orecv.at[g, zh], o_recv_sem.at[g]).start()
    pltpu.make_async_copy(ssend.at[g, zh], srecv.at[g, zh], s_recv_sem.at[g]).start()

    c_lane = lax.broadcasted_iota(jnp.int32, (qn, head), 1)
    c_row = lax.broadcasted_iota(jnp.int32, (qn, head), 0)

    def combine(i, _):
        src = towards(i)
        pltpu.make_async_copy(orecv.at[src], orecv.at[src], o_recv_sem.at[src]).wait()
        pltpu.make_async_copy(srecv.at[src], srecv.at[src], s_recv_sem.at[src]).wait()
        m, l, o = [fm[src]], [fl[src]], [fo[src]]
        for h in range(ZH):
            stat = jnp.broadcast_to(srecv[src, h], (qn, head))
            m.append(jnp.sum(jnp.where(c_lane == c_row, stat, 0.0), axis=1, keepdims=True))
            l.append(jnp.sum(jnp.where(c_lane == c_row + qn, stat, 0.0), axis=1, keepdims=True))
            o.append(orecv[src, h].astype(jnp.float32))
        top = functools.reduce(jnp.maximum, m)
        w = [jnp.exp(a - top) for a in m]
        den = sum(a * b for a, b in zip(w, l))
        num = sum(a * b for a, b in zip(w, o))
        out_ref[src] = (num / den).astype(jnp.bfloat16)
        return 0

    lax.fori_loop(0, groups, combine, 0)

    for c in range(CHUNKS):
        for k in range(1, ys):
            kv_copy(k, c).wait_send()
    for ref, sem in ((qbuf, q_send_sem), (osend, o_send_sem), (ssend, s_send_sem)):
        pltpu.make_async_copy(ref.at[pl.ds(0, last)], ref.at[pl.ds(0, last)], sem).wait()
        pltpu.make_async_copy(ref.at[last, 0], ref.at[last, 0], sem).wait()


def shards(cache_blocks, prompt_len, dest_perm, new_q, new_kv):
    groups = lax.axis_size("group")
    tensors = lax.axis_size("tensor")
    own = lax.axis_index("group")
    requests, _, tok, heads, width = cache_blocks.shape
    head = width // 2
    slots, steps, q_here = new_q.shape[1:4]
    qn = steps * q_here
    ids = jnp.arange(groups, dtype=jnp.int32)
    order = lax.dynamic_index_in_dim(dest_perm, own, 0, keepdims=False)
    lens = lax.dynamic_index_in_dim(prompt_len, own, 0, keepdims=False)
    match = order[:, None] == ids[None, :]
    position = jnp.sum(jnp.where(match, ids[:, None], 0), axis=0)
    length = jnp.sum(jnp.where(match, lens[:, None], 0), axis=0)
    cache = cache_blocks.reshape(requests, tok * heads, width)
    queries = new_q.reshape(slots, qn, head)
    fresh = new_kv.reshape(CHUNKS, slots // CHUNKS * steps, width)
    ys = tensors // ZH
    piece = ZH * tok
    bf16, f32 = jnp.bfloat16, jnp.float32
    vmem = pl.BlockSpec(memory_space=pltpu.VMEM)
    smem = pl.BlockSpec(memory_space=pltpu.SMEM)
    dma = pltpu.SemaphoreType.DMA
    out = pl.pallas_call(
        functools.partial(kernel, groups, tensors),
        out_shape=jax.ShapeDtypeStruct((slots, qn, head), bf16),
        in_specs=[pl.BlockSpec(memory_space=pl.ANY), smem, smem, vmem, vmem],
        out_specs=vmem,
        scratch_shapes=[
            pltpu.VMEM((requests, tok * heads, width), bf16),
            pltpu.VMEM((ys - 1, requests, piece, width), bf16),
            pltpu.VMEM((requests, ys, piece, width), bf16),
            pltpu.VMEM((groups, ZH, qn, head), bf16),
            pltpu.VMEM((groups, ZH, qn, head), bf16),
            pltpu.VMEM((groups, ZH, qn, head), bf16),
            pltpu.VMEM((groups, ZH, 1, head), f32),
            pltpu.VMEM((groups, ZH, 1, head), f32),
            pltpu.VMEM((slots, qn, head), f32),
            pltpu.VMEM((slots, qn, head), f32),
            pltpu.VMEM((slots, qn, head), f32),
            dma((CHUNKS,)),
            dma((ys - 1, CHUNKS)),
            dma((ys - 1, CHUNKS)),
            dma,
            dma((groups,)),
            dma,
            dma((groups,)),
            dma,
            dma((groups,)),
        ],
        compiler_params=pltpu.CompilerParams(
            collective_id=0, has_side_effects=True, vmem_limit_bytes=48 << 20),
        cost_estimate=pl.CostEstimate(flops=1 << 30, bytes_accessed=12 << 20, transcendentals=1 << 20),
    )(cache, position, length, queries, fresh)
    return out.reshape(1, slots, steps, q_here, head)


def solution(mesh):
    placed = (
        P("group", None, "tensor", None, None),
        P(),
        P(),
        P("group", None, None, "tensor", None),
        P("group", None, None, "tensor", None),
    )
    return jax.shard_map(
        shards,
        mesh=mesh,
        in_specs=placed,
        out_specs=P("group", None, None, "tensor", None),
        check_vma=False,
    )
```

```python
import functools
import math

import jax
import jax.numpy as jnp
from jax import lax
from jax.experimental import pallas as pl
from jax.experimental.pallas import tpu as pltpu
from jax.sharding import PartitionSpec as P

MESH = pl.DeviceIdType.MESH

X, ZL, CORES = 4, 8, 2
ZH = 2
CHUNKS = 8
NONE = -1e30


def kernel(groups, tensors, cache_ref, perm_ref, plen_ref, newq_ref, newkv_ref, out_ref,
           cbuf, q_ref, fresh_ref, perm_v, plen_v, meta, where_ref, kvsend, kvrecv, qbuf, osend, orecv, ssend, srecv, fo, fm, fl,
           cache_sem, in_sem, meet_sem, kv_send_sem, kv_recv_sem, q_send_sem, q_recv_sem,
           o_send_sem, o_recv_sem, s_send_sem, s_recv_sem):
    ys = tensors // ZH
    zs = ZH * ZL
    plane = X * CORES
    g = lax.axis_index("group")
    t = lax.axis_index("tensor")
    y, zh = t // ZH, t % ZH
    core, zl, x = g % CORES, (g // CORES) % ZL, g // (CORES * ZL)
    z = zh * ZL + zl
    rows, qn, head = q_ref.shape
    steps = fresh_ref.shape[1]
    tok = cache_ref.shape[1] // tensors
    piece = ZH * tok
    per = rows // CHUNKS
    scale = 1.0 / math.sqrt(head)
    last = groups - 1

    def group_of(px, pz, pc):
        return (px * ZL + pz % ZL) * CORES + pc

    def tensor_of(pz):
        return y * ZH + pz // ZL

    def ahead(dx, dz, dc):
        return (x + dx) % X, (z + dz) % zs, (core + dc) % CORES

    def q_target(i):
        k, j = i // plane, plane - 1 - i % plane
        far = (zs // 2 + (1 - 2 * (k % 2)) * ((k + 1) // 2)) % zs
        return ahead(j // CORES, far, j % CORES)

    def step_offset(i):
        j = plane - 1 - i // ZL
        k = (i + j) % ZL
        far = ZL // 2 + (k // 2) * (1 - k % 2) - ((k + 1) // 2) * (k % 2)
        return j // CORES, far, j % CORES

    def towards(i):
        dx, dz, dc = step_offset(i)
        return (((x + dx) % X) * ZL + (zl + dz) % ZL) * CORES + (core + dc) % CORES

    def source(i):
        dx, dz, dc = step_offset(i)
        return (((x + X - dx) % X) * ZL + (zl + ZL - dz) % ZL) * CORES + (core + CORES - dc) % CORES

    def cache_copy(c):
        return pltpu.make_async_copy(
            cache_ref.at[pl.ds(c * per, per)], cbuf.at[pl.ds(c * per, per)], cache_sem.at[c])

    staged = [
        pltpu.make_async_copy(src, dst, in_sem.at[n])
        for n, (src, dst) in enumerate(
            ((newq_ref, q_ref), (newkv_ref, fresh_ref), (perm_ref, perm_v), (plen_ref, plen_v)))
    ]
    cache_copy(0).start()
    staged[0].start()
    for c in range(1, CHUNKS):
        cache_copy(c).start()
    for copy in staged[1:]:
        copy.start()

    barrier = pltpu.get_barrier_semaphore()

    def greet(sem, px, pz, pc):
        pl.semaphore_signal(
            sem, inc=1, device_id=(group_of(px, pz, pc), tensor_of(pz)), device_id_type=MESH)

    for k in range(1, ys):
        pl.semaphore_signal(barrier, inc=1, device_id=(g, ((y + k) % ys) * ZH + zh), device_id_type=MESH)
    for dz in range(1, zs):
        greet(barrier, *ahead(0, dz, 0))
    for j in range(1, plane):
        greet(barrier, *ahead(j // CORES, 0, j % CORES))

    size = tensors * tok
    r_out = lax.broadcasted_iota(jnp.int32, (size, size), 0)
    r_in = lax.broadcasted_iota(jnp.int32, (size, size), 1)
    pair = r_out // piece + y
    pair = jnp.where(pair >= ys, pair - ys, pair)
    wanted = (r_out % tok) * tensors + pair * ZH + (r_out % piece) // tok
    shuffle = jnp.where(wanted == r_in, 1.0, 0.0).astype(jnp.bfloat16)

    def kv_copy(k, c):
        return pltpu.make_async_remote_copy(
            src_ref=kvsend.at[k - 1, pl.ds(c * per, per)],
            dst_ref=kvrecv.at[pl.ds(c * per, per), y],
            send_sem=kv_send_sem.at[k - 1, c], recv_sem=kv_recv_sem.at[k - 1, c],
            device_id=(g, ((y + k) % ys) * ZH + zh), device_id_type=MESH)

    def regroup(c):
        cache_copy(c).wait()

        def one(i, _):
            for u in range(2):
                r = c * per + i * 2 + u
                moved = jnp.dot(shuffle, cbuf[r], preferred_element_type=jnp.float32).astype(jnp.bfloat16)
                kvrecv[r, y] = moved[:piece]
                for k in range(1, ys):
                    kvsend[k - 1, r] = moved[k * piece:(k + 1) * piece]
            return 0

        lax.fori_loop(0, per // 2, one, 0)

    def send_kv(c):
        for k in range(1, ys):
            kv_copy(k, c).start()

    def q_copy(peer, tensor):
        return pltpu.make_async_remote_copy(
            src_ref=q_ref.at[peer], dst_ref=qbuf.at[g, zh], send_sem=q_send_sem,
            recv_sem=q_recv_sem.at[g], device_id=(peer, tensor), device_id_type=MESH)

    def send_q(i, _):
        px, pz, pc = q_target(i)
        q_copy(group_of(px, pz, pc), tensor_of(pz)).start()
        return 0

    regroup(0)
    pl.semaphore_wait(barrier, ys - 1 + zs - 1 + plane - 1)
    for j in range(1, plane):
        greet(meet_sem, *ahead(j // CORES, 0, j % CORES))
    send_kv(0)
    staged[0].wait()
    regroup(1)
    send_kv(1)
    pl.semaphore_wait(meet_sem, plane - 1)
    pltpu.make_async_copy(q_ref.at[g], qbuf.at[g, zh], q_recv_sem.at[g]).start()
    queries = zs * plane - 1
    share = -(-queries // max(CHUNKS - 2, 1))
    done = 0
    for c in range(2, CHUNKS):
        lax.fori_loop(done, min(done + share, queries), send_q, 0)
        done = min(done + share, queries)
        regroup(c)
        send_kv(c)
    lax.fori_loop(done, queries, send_q, 0)

    staged[2].wait()
    staged[3].wait()
    square = (groups, rows)
    down = lax.broadcasted_iota(jnp.int32, square, 0)
    along = lax.broadcasted_iota(jnp.int32, square, 1)

    def column(ref):
        row = jnp.broadcast_to(ref[pl.ds(g, 1), :], square)
        return jnp.sum(jnp.where(down == along, row, 0), axis=1, keepdims=True)

    match = column(perm_v) == along
    position = jnp.sum(jnp.where(match, down, 0), axis=0, keepdims=True)
    length = jnp.sum(jnp.where(match, column(plen_v), 0), axis=0, keepdims=True)
    meta[0:1, 0:groups] = jnp.minimum(position, rows - 1)
    meta[1:2, 0:groups] = jnp.where(position < rows, length, 0)
    to_scalar = pltpu.make_async_copy(meta, where_ref, in_sem.at[2])
    to_scalar.start()

    staged[1].wait()
    at = per
    shape = (at, qn, steps)
    f_keep = lax.broadcasted_iota(jnp.int32, shape, 2) <= lax.broadcasted_iota(jnp.int32, shape, 1) // (qn // steps)

    def fresh_part(b, _):
        q = q_ref[pl.ds(b * at, at)]
        kv = fresh_ref[pl.ds(b * at, at)]
        s = jnp.einsum("bqd,bud->bqu", q, kv[:, :, :head], preferred_element_type=jnp.float32) * scale
        s = jnp.where(f_keep, s, NONE)
        m = jnp.max(s, axis=2, keepdims=True)
        p = jnp.exp(s - m)
        l = jnp.sum(p, axis=2, keepdims=True)
        o = jnp.einsum("bqu,bud->bqd", p.astype(jnp.bfloat16), kv[:, :, head:], preferred_element_type=jnp.float32)
        fo[pl.ds(b * at, at)] = o
        fm[pl.ds(b * at, at)] = jnp.broadcast_to(m, (at, qn, head))
        fl[pl.ds(b * at, at)] = jnp.broadcast_to(l, (at, qn, head))
        return 0

    lax.fori_loop(0, rows // at, fresh_part, 0)
    to_scalar.wait()

    for c in range(CHUNKS):
        for k in range(1, ys):
            kv_copy(k, c).wait_recv()

    both = ZH * qn
    shape = (both, ys * piece)
    a_row = lax.broadcasted_iota(jnp.int32, shape, 0)
    a_col = lax.broadcasted_iota(jnp.int32, shape, 1)
    token = ((a_col // piece) * ZH + zh) * tok + a_col % tok
    token = jnp.where((a_col % piece) // tok == a_row // qn, token, 1 << 20)
    lane = lax.broadcasted_iota(jnp.int32, (both, head), 1)
    diag = lax.broadcasted_iota(jnp.int32, (both, head), 0) % qn
    on_m, on_l = lane == diag, lane == diag + qn

    def o_copy(peer, h):
        return pltpu.make_async_remote_copy(
            src_ref=osend.at[peer, h], dst_ref=orecv.at[g, zh], send_sem=o_send_sem,
            recv_sem=o_recv_sem.at[g], device_id=(peer, y * ZH + h), device_id_type=MESH)

    def s_copy(peer, h):
        return pltpu.make_async_remote_copy(
            src_ref=ssend.at[peer, h], dst_ref=srecv.at[g, zh], send_sem=s_send_sem,
            recv_sem=s_recv_sem.at[g], device_id=(peer, y * ZH + h), device_id_type=MESH)

    def attend(i):
        src = source(i)
        pltpu.make_async_copy(qbuf.at[src], qbuf.at[src], q_recv_sem.at[src]).wait()
        q = qbuf[src].reshape(both, head)
        kv = kvrecv[where_ref[0, src]].reshape(ys * piece, 2 * head)
        s = lax.dot_general(q, kv[:, :head], (((1,), (1,)), ((), ())), preferred_element_type=jnp.float32) * scale
        keep = token < where_ref[1, src]
        s = jnp.where(keep, s, NONE)
        m = jnp.max(s, axis=1, keepdims=True)
        p = jnp.where(keep, jnp.exp(s - m), 0.0)
        l = jnp.sum(p, axis=1, keepdims=True)
        o = jnp.dot(p.astype(jnp.bfloat16), kv[:, head:], preferred_element_type=jnp.float32)
        osend[src] = o.astype(jnp.bfloat16).reshape(ZH, qn, head)
        stat = jnp.where(on_m, m, jnp.where(on_l, l, 0.0))
        ssend[src] = jnp.sum(stat.reshape(ZH, qn, head), axis=1, keepdims=True)
        return src

    def attend_send(i, _):
        src = attend(i)
        for h in range(ZH):
            s_copy(src, h).start()
            o_copy(src, h).start()
        return 0

    lax.fori_loop(0, last, attend_send, 0)
    attend(last)
    s_copy(g, 1 - zh).start()
    o_copy(g, 1 - zh).start()
    pltpu.make_async_copy(osend.at[g, zh], orecv.at[g, zh], o_recv_sem.at[g]).start()
    pltpu.make_async_copy(ssend.at[g, zh], srecv.at[g, zh], s_recv_sem.at[g]).start()

    c_lane = lax.broadcasted_iota(jnp.int32, (qn, head), 1)
    c_row = lax.broadcasted_iota(jnp.int32, (qn, head), 0)

    def combine(i, _):
        src = towards(i)
        pltpu.make_async_copy(srecv.at[src], srecv.at[src], s_recv_sem.at[src]).wait()
        pltpu.make_async_copy(orecv.at[src], orecv.at[src], o_recv_sem.at[src]).wait()
        m, l, o = [fm[src]], [fl[src]], [fo[src]]
        for h in range(ZH):
            stat = jnp.broadcast_to(srecv[src, h], (qn, head))
            m.append(jnp.sum(jnp.where(c_lane == c_row, stat, 0.0), axis=1, keepdims=True))
            l.append(jnp.sum(jnp.where(c_lane == c_row + qn, stat, 0.0), axis=1, keepdims=True))
            o.append(orecv[src, h].astype(jnp.float32))
        top = functools.reduce(jnp.maximum, m)
        w = [jnp.exp(a - top) for a in m]
        den = sum(a * b for a, b in zip(w, l))
        num = sum(a * b for a, b in zip(w, o))
        out_ref[src] = (num / den).astype(jnp.bfloat16)
        return 0

    lax.fori_loop(0, groups, combine, 0)

    for c in range(CHUNKS):
        for k in range(1, ys):
            kv_copy(k, c).wait_send()
    for ref, sem in ((qbuf, q_send_sem), (osend, o_send_sem), (ssend, s_send_sem)):
        pltpu.make_async_copy(ref.at[pl.ds(0, last)], ref.at[pl.ds(0, last)], sem).wait()
        pltpu.make_async_copy(ref.at[last, 0], ref.at[last, 0], sem).wait()


def shards(cache_blocks, prompt_len, dest_perm, new_q, new_kv):
    groups = lax.axis_size("group")
    tensors = lax.axis_size("tensor")
    requests, _, tok, heads, width = cache_blocks.shape
    head = width // 2
    slots, steps, q_here = new_q.shape[1:4]
    qn = steps * q_here
    cache = cache_blocks.reshape(requests, tok * heads, width)
    queries = new_q.reshape(slots, qn, head)
    fresh = new_kv.reshape(slots, steps, width)
    ys = tensors // ZH
    piece = ZH * tok
    bf16, f32, i32 = jnp.bfloat16, jnp.float32, jnp.int32
    anywhere = pl.BlockSpec(memory_space=pl.ANY)
    dma = pltpu.SemaphoreType.DMA
    out = pl.pallas_call(
        functools.partial(kernel, groups, tensors),
        out_shape=jax.ShapeDtypeStruct((slots, qn, head), bf16),
        in_specs=[anywhere] * 5,
        out_specs=pl.BlockSpec(memory_space=pltpu.VMEM),
        scratch_shapes=[
            pltpu.VMEM((requests, tok * heads, width), bf16),
            pltpu.VMEM((slots, qn, head), bf16),
            pltpu.VMEM((slots, steps, width), bf16),
            pltpu.VMEM(dest_perm.shape, i32),
            pltpu.VMEM(prompt_len.shape, i32),
            pltpu.VMEM((8, 128), i32),
            pltpu.SMEM((8, 128), i32),
            pltpu.VMEM((ys - 1, requests, piece, width), bf16),
            pltpu.VMEM((requests, ys, piece, width), bf16),
            pltpu.VMEM((groups, ZH, qn, head), bf16),
            pltpu.VMEM((groups, ZH, qn, head), bf16),
            pltpu.VMEM((groups, ZH, qn, head), bf16),
            pltpu.VMEM((groups, ZH, 1, head), f32),
            pltpu.VMEM((groups, ZH, 1, head), f32),
            pltpu.VMEM((slots, qn, head), f32),
            pltpu.VMEM((slots, qn, head), f32),
            pltpu.VMEM((slots, qn, head), f32),
            dma((CHUNKS,)),
            dma((4,)),
            pltpu.SemaphoreType.REGULAR,
            dma((ys - 1, CHUNKS)),
            dma((ys - 1, CHUNKS)),
            dma,
            dma((groups,)),
            dma,
            dma((groups,)),
            dma,
            dma((groups,)),
        ],
        compiler_params=pltpu.CompilerParams(
            collective_id=0, has_side_effects=True, vmem_limit_bytes=58 << 20),
        cost_estimate=pl.CostEstimate(flops=1 << 30, bytes_accessed=12 << 20, transcendentals=1 << 20),
    )(cache, dest_perm, prompt_len, queries, fresh)
    return out.reshape(1, slots, steps, q_here, head)


def solution(mesh):
    placed = (
        P("group", None, "tensor", None, None),
        P(),
        P(),
        P("group", None, None, "tensor", None),
        P("group", None, None, "tensor", None),
    )
    return jax.shard_map(
        shards,
        mesh=mesh,
        in_specs=placed,
        out_specs=P("group", None, None, "tensor", None),
        check_vma=False,
    )
```

```python
import functools
import math

import jax
import jax.numpy as jnp
from jax import lax
from jax.experimental import pallas as pl
from jax.experimental.pallas import tpu as pltpu
from jax.sharding import PartitionSpec as P

MESH = pl.DeviceIdType.MESH

X, ZL, CORES = 4, 8, 2
ZH = 2
CHUNKS = 8
NONE = -1e30


def kernel(groups, tensors, cache_ref, perm_ref, plen_ref, newq_ref, newkv_ref, out_ref,
           cbuf, q_ref, fresh_ref, perm_v, plen_v, meta, where_ref, kvsend, kvrecv, qbuf, osend, orecv, ssend, srecv, fo, fm, fl,
           cache_sem, in_sem, meet_sem, kv_send_sem, kv_recv_sem, q_send_sem, q_recv_sem,
           o_send_sem, o_recv_sem, s_send_sem, s_recv_sem):
    ys = tensors // ZH
    zs = ZH * ZL
    plane = X * CORES
    g = lax.axis_index("group")
    t = lax.axis_index("tensor")
    y, zh = t // ZH, t % ZH
    core, zl, x = g % CORES, (g // CORES) % ZL, g // (CORES * ZL)
    z = zh * ZL + zl
    rows, qn, head = q_ref.shape
    steps = fresh_ref.shape[1]
    tok = cache_ref.shape[1] // tensors
    piece = ZH * tok
    per = rows // CHUNKS
    scale = 1.0 / math.sqrt(head)
    last = groups - 1

    def group_of(px, pz, pc):
        return (px * ZL + pz % ZL) * CORES + pc

    def tensor_of(pz):
        return y * ZH + pz // ZL

    def ahead(dx, dz, dc):
        return (x + dx) % X, (z + dz) % zs, (core + dc) % CORES

    def step_offset(i):
        n = (i + 1) % groups
        j = n // ZL
        k = ZL - 1 - (n + j) % ZL
        far = ZL // 2 + (k // 2) * (1 - k % 2) - ((k + 1) // 2) * (k % 2)
        return j // CORES, far, j % CORES

    def towards(i):
        dx, dz, dc = step_offset(i)
        return (((x + dx) % X) * ZL + (zl + dz) % ZL) * CORES + (core + dc) % CORES

    def source(i):
        dx, dz, dc = step_offset(i)
        return (((x + X - dx) % X) * ZL + (zl + ZL - dz) % ZL) * CORES + (core + CORES - dc) % CORES

    def cache_copy(c):
        return pltpu.make_async_copy(
            cache_ref.at[pl.ds(c * per, per)], cbuf.at[pl.ds(c * per, per)], cache_sem.at[c])

    staged = [
        pltpu.make_async_copy(src, dst, in_sem.at[n])
        for n, (src, dst) in enumerate(
            ((newq_ref, q_ref), (newkv_ref, fresh_ref), (perm_ref, perm_v), (plen_ref, plen_v)))
    ]
    for copy in staged[2:]:
        copy.start()
    for c in range(CHUNKS):
        cache_copy(c).start()
    for copy in staged[:2]:
        copy.start()

    barrier = pltpu.get_barrier_semaphore()

    def greet(sem, px, pz, pc):
        pl.semaphore_signal(
            sem, inc=1, device_id=(group_of(px, pz, pc), tensor_of(pz)), device_id_type=MESH)

    for k in range(1, ys):
        pl.semaphore_signal(barrier, inc=1, device_id=(g, ((y + k) % ys) * ZH + zh), device_id_type=MESH)
    for dz in range(1, zs):
        greet(barrier, *ahead(0, dz, 0))
    for j in range(1, plane):
        greet(barrier, *ahead(j // CORES, 0, j % CORES))

    staged[2].wait()
    staged[3].wait()
    square = (groups, rows)
    down = lax.broadcasted_iota(jnp.int32, square, 0)
    along = lax.broadcasted_iota(jnp.int32, square, 1)

    def column(ref):
        row = jnp.broadcast_to(ref[pl.ds(g, 1), :], square)
        return jnp.sum(jnp.where(down == along, row, 0), axis=1, keepdims=True)

    match = column(perm_v) == along
    position = jnp.sum(jnp.where(match, down, 0), axis=0, keepdims=True)
    length = jnp.sum(jnp.where(match, column(plen_v), 0), axis=0, keepdims=True)
    meta[0:1, 0:groups] = jnp.minimum(position, rows - 1)
    meta[1:2, 0:groups] = jnp.where(position < rows, length, 0)
    to_scalar = pltpu.make_async_copy(meta, where_ref, in_sem.at[2])
    to_scalar.start()

    size = tensors * tok
    r_out = lax.broadcasted_iota(jnp.int32, (size, size), 0)
    r_in = lax.broadcasted_iota(jnp.int32, (size, size), 1)
    pair = r_out // piece + y
    pair = jnp.where(pair >= ys, pair - ys, pair)
    wanted = (r_out % tok) * tensors + pair * ZH + (r_out % piece) // tok
    shuffle = jnp.where(wanted == r_in, 1.0, 0.0).astype(jnp.bfloat16)

    def kv_copy(k, c):
        return pltpu.make_async_remote_copy(
            src_ref=kvsend.at[k - 1, pl.ds(c * per, per)],
            dst_ref=kvrecv.at[pl.ds(c * per, per), y],
            send_sem=kv_send_sem.at[k - 1, c], recv_sem=kv_recv_sem.at[k - 1, c],
            device_id=(g, ((y + k) % ys) * ZH + zh), device_id_type=MESH)

    def regroup(c):
        def one(i, _):
            for u in range(2):
                r = c * per + i * 2 + u
                cache = cbuf[where_ref[0, source(r)]]
                moved = jnp.dot(shuffle, cache, preferred_element_type=jnp.float32).astype(jnp.bfloat16)
                kvrecv[r, y] = moved[:piece]
                for k in range(1, ys):
                    kvsend[k - 1, r] = moved[k * piece:(k + 1) * piece]
            return 0

        lax.fori_loop(0, per // 2, one, 0)

    def send_kv(c):
        for k in range(1, ys):
            kv_copy(k, c).start()

    def q_copy(peer, tensor):
        return pltpu.make_async_remote_copy(
            src_ref=q_ref.at[peer], dst_ref=qbuf.at[g, zh], send_sem=q_send_sem,
            recv_sem=q_recv_sem.at[g], device_id=(peer, tensor), device_id_type=MESH)

    def send_q(i, _):
        peer = towards(i)
        for h in range(ZH):
            q_copy(peer, y * ZH + h).start()
        return 0

    to_scalar.wait()
    for c in range(CHUNKS):
        cache_copy(c).wait()
    regroup(0)
    staged[0].wait()
    pltpu.make_async_copy(q_ref.at[g], qbuf.at[g, zh], q_recv_sem.at[g]).start()
    pl.semaphore_wait(barrier, ys - 1 + zs - 1 + plane - 1)
    for j in range(1, plane):
        greet(meet_sem, *ahead(j // CORES, 0, j % CORES))
    line = ZL - 1
    lax.fori_loop(0, line, send_q, 0)
    q_copy(g, y * ZH + 1 - zh).start()
    send_kv(0)
    regroup(1)
    send_kv(1)
    pl.semaphore_wait(meet_sem, plane - 1)
    done = line
    for c in range(2, CHUNKS):
        upto = line + (last - line) * (c - 1) // (CHUNKS - 2)
        lax.fori_loop(done, upto, send_q, 0)
        done = upto
        regroup(c)
        send_kv(c)
    lax.fori_loop(done, last, send_q, 0)

    staged[1].wait()
    at = per
    shape = (at, qn, steps)
    f_keep = lax.broadcasted_iota(jnp.int32, shape, 2) <= lax.broadcasted_iota(jnp.int32, shape, 1) // (qn // steps)

    def fresh_part(b, _):
        q = q_ref[pl.ds(b * at, at)]
        kv = fresh_ref[pl.ds(b * at, at)]
        s = jnp.einsum("bqd,bud->bqu", q, kv[:, :, :head], preferred_element_type=jnp.float32) * scale
        s = jnp.where(f_keep, s, NONE)
        m = jnp.max(s, axis=2, keepdims=True)
        p = jnp.exp(s - m)
        l = jnp.sum(p, axis=2, keepdims=True)
        o = jnp.einsum("bqu,bud->bqd", p.astype(jnp.bfloat16), kv[:, :, head:], preferred_element_type=jnp.float32)
        fo[pl.ds(b * at, at)] = o
        fm[pl.ds(b * at, at)] = jnp.broadcast_to(m, (at, qn, head))
        fl[pl.ds(b * at, at)] = jnp.broadcast_to(l, (at, qn, head))
        return 0

    lax.fori_loop(0, rows // at, fresh_part, 0)

    both = ZH * qn
    shape = (both, ys * piece)
    a_row = lax.broadcasted_iota(jnp.int32, shape, 0)
    a_col = lax.broadcasted_iota(jnp.int32, shape, 1)
    token = ((a_col // piece) * ZH + zh) * tok + a_col % tok
    token = jnp.where((a_col % piece) // tok == a_row // qn, token, 1 << 20)
    lane = lax.broadcasted_iota(jnp.int32, (both, head), 1)
    diag = lax.broadcasted_iota(jnp.int32, (both, head), 0) % qn
    on_m, on_l = lane == diag, lane == diag + qn

    def o_copy(peer, h):
        return pltpu.make_async_remote_copy(
            src_ref=osend.at[peer, h], dst_ref=orecv.at[g, zh], send_sem=o_send_sem,
            recv_sem=o_recv_sem.at[g], device_id=(peer, y * ZH + h), device_id_type=MESH)

    def s_copy(peer, h):
        return pltpu.make_async_remote_copy(
            src_ref=ssend.at[peer, h], dst_ref=srecv.at[g, zh], send_sem=s_send_sem,
            recv_sem=s_recv_sem.at[g], device_id=(peer, y * ZH + h), device_id_type=MESH)

    def attend(i):
        src = source(i)
        pltpu.make_async_copy(qbuf.at[src], qbuf.at[src], q_recv_sem.at[src]).wait()
        q = qbuf[src].reshape(both, head)
        kv = kvrecv[i].reshape(ys * piece, 2 * head)
        s = lax.dot_general(q, kv[:, :head], (((1,), (1,)), ((), ())), preferred_element_type=jnp.float32) * scale
        keep = token < where_ref[1, src]
        s = jnp.where(keep, s, NONE)
        m = jnp.max(s, axis=1, keepdims=True)
        p = jnp.where(keep, jnp.exp(s - m), 0.0)
        l = jnp.sum(p, axis=1, keepdims=True)
        o = jnp.dot(p.astype(jnp.bfloat16), kv[:, head:], preferred_element_type=jnp.float32)
        osend[src] = o.astype(jnp.bfloat16).reshape(ZH, qn, head)
        stat = jnp.where(on_m, m, jnp.where(on_l, l, 0.0))
        ssend[src] = jnp.sum(stat.reshape(ZH, qn, head), axis=1, keepdims=True)
        return src

    def attend_send(i, _):
        src = attend(i)
        for h in range(ZH):
            s_copy(src, h).start()
            o_copy(src, h).start()
        return 0

    for c in range(CHUNKS):
        for k in range(1, ys):
            kv_copy(k, c).wait_recv()
        lax.fori_loop(c * per, min((c + 1) * per, last), attend_send, 0)
    attend(last)
    s_copy(g, 1 - zh).start()
    o_copy(g, 1 - zh).start()
    pltpu.make_async_copy(osend.at[g, zh], orecv.at[g, zh], o_recv_sem.at[g]).start()
    pltpu.make_async_copy(ssend.at[g, zh], srecv.at[g, zh], s_recv_sem.at[g]).start()

    c_lane = lax.broadcasted_iota(jnp.int32, (qn, head), 1)
    c_row = lax.broadcasted_iota(jnp.int32, (qn, head), 0)

    def combine(i, _):
        src = towards(i)
        pltpu.make_async_copy(srecv.at[src], srecv.at[src], s_recv_sem.at[src]).wait()
        pltpu.make_async_copy(orecv.at[src], orecv.at[src], o_recv_sem.at[src]).wait()
        m, l, o = [fm[src]], [fl[src]], [fo[src]]
        for h in range(ZH):
            stat = jnp.broadcast_to(srecv[src, h], (qn, head))
            m.append(jnp.sum(jnp.where(c_lane == c_row, stat, 0.0), axis=1, keepdims=True))
            l.append(jnp.sum(jnp.where(c_lane == c_row + qn, stat, 0.0), axis=1, keepdims=True))
            o.append(orecv[src, h].astype(jnp.float32))
        top = functools.reduce(jnp.maximum, m)
        w = [jnp.exp(a - top) for a in m]
        den = sum(a * b for a, b in zip(w, l))
        num = sum(a * b for a, b in zip(w, o))
        out_ref[src] = (num / den).astype(jnp.bfloat16)
        return 0

    lax.fori_loop(0, groups, combine, 0)

    for c in range(CHUNKS):
        for k in range(1, ys):
            kv_copy(k, c).wait_send()
    for ref, sem in ((qbuf, q_send_sem), (osend, o_send_sem), (ssend, s_send_sem)):
        pltpu.make_async_copy(ref.at[pl.ds(0, last)], ref.at[pl.ds(0, last)], sem).wait()
        pltpu.make_async_copy(ref.at[last, 0], ref.at[last, 0], sem).wait()


def shards(cache_blocks, prompt_len, dest_perm, new_q, new_kv):
    groups = lax.axis_size("group")
    tensors = lax.axis_size("tensor")
    requests, _, tok, heads, width = cache_blocks.shape
    head = width // 2
    slots, steps, q_here = new_q.shape[1:4]
    qn = steps * q_here
    cache = cache_blocks.reshape(requests, tok * heads, width)
    queries = new_q.reshape(slots, qn, head)
    fresh = new_kv.reshape(slots, steps, width)
    ys = tensors // ZH
    piece = ZH * tok
    bf16, f32, i32 = jnp.bfloat16, jnp.float32, jnp.int32
    hbm = pl.BlockSpec(memory_space=pltpu.HBM)
    dma = pltpu.SemaphoreType.DMA
    out = pl.pallas_call(
        functools.partial(kernel, groups, tensors),
        out_shape=jax.ShapeDtypeStruct((slots, qn, head), bf16),
        in_specs=[hbm] * 5,
        out_specs=pl.BlockSpec(memory_space=pltpu.VMEM),
        scratch_shapes=[
            pltpu.VMEM((requests, tok * heads, width), bf16),
            pltpu.VMEM((slots, qn, head), bf16),
            pltpu.VMEM((slots, steps, width), bf16),
            pltpu.VMEM(dest_perm.shape, i32),
            pltpu.VMEM(prompt_len.shape, i32),
            pltpu.VMEM((8, 128), i32),
            pltpu.SMEM((8, 128), i32),
            pltpu.VMEM((ys - 1, requests, piece, width), bf16),
            pltpu.VMEM((requests, ys, piece, width), bf16),
            pltpu.VMEM((groups, ZH, qn, head), bf16),
            pltpu.VMEM((groups, ZH, qn, head), bf16),
            pltpu.VMEM((groups, ZH, qn, head), bf16),
            pltpu.VMEM((groups, ZH, 1, head), f32),
            pltpu.VMEM((groups, ZH, 1, head), f32),
            pltpu.VMEM((slots, qn, head), f32),
            pltpu.VMEM((slots, qn, head), f32),
            pltpu.VMEM((slots, qn, head), f32),
            dma((CHUNKS,)),
            dma((4,)),
            pltpu.SemaphoreType.REGULAR,
            dma((ys - 1, CHUNKS)),
            dma((ys - 1, CHUNKS)),
            dma,
            dma((groups,)),
            dma,
            dma((groups,)),
            dma,
            dma((groups,)),
        ],
        compiler_params=pltpu.CompilerParams(
            collective_id=0, has_side_effects=True, vmem_limit_bytes=48 << 20),
        cost_estimate=pl.CostEstimate(flops=1 << 30, bytes_accessed=12 << 20, transcendentals=1 << 20),
    )(*(pltpu.with_memory_space_constraint(a, pltpu.HBM) for a in (cache, dest_perm, prompt_len, queries, fresh)))
    return out.reshape(1, slots, steps, q_here, head)


def solution(mesh):
    placed = (
        P("group", None, "tensor", None, None),
        P(),
        P(),
        P("group", None, None, "tensor", None),
        P("group", None, None, "tensor", None),
    )
    return jax.shard_map(
        shards,
        mesh=mesh,
        in_specs=placed,
        out_specs=P("group", None, None, "tensor", None),
        check_vma=False,
    )
```

```python
import functools
import math

import jax
import jax.numpy as jnp
from jax import lax
from jax.experimental import pallas as pl
from jax.experimental.pallas import tpu as pltpu
from jax.sharding import PartitionSpec as P

MESH = pl.DeviceIdType.MESH

X, ZL, CORES = 4, 8, 2
ZH = 2
CHUNKS = 8
NONE = -1e30


def kernel(groups, tensors, cache_ref, perm_ref, plen_ref, newq_ref, newkv_ref, out_ref,
           cbuf, q_ref, fresh_ref, perm_v, plen_v, meta, where_ref, kvsend, kvrecv, qbuf, osend, orecv, ssend, srecv, fo, fm, fl,
           cache_sem, in_sem, meet_sem, kv_send_sem, kv_recv_sem, q_send_sem, q_recv_sem,
           o_send_sem, o_recv_sem, s_send_sem, s_recv_sem):
    ys = tensors // ZH
    zs = ZH * ZL
    plane = X * CORES
    g = lax.axis_index("group")
    t = lax.axis_index("tensor")
    y, zh = t // ZH, t % ZH
    core, zl, x = g % CORES, (g // CORES) % ZL, g // (CORES * ZL)
    z = zh * ZL + zl
    rows, qn, head = q_ref.shape
    steps = fresh_ref.shape[1]
    tok = cache_ref.shape[1] // tensors
    piece = ZH * tok
    per = rows // CHUNKS
    scale = 1.0 / math.sqrt(head)
    last = groups - 1

    def group_of(px, pz, pc):
        return (px * ZL + pz % ZL) * CORES + pc

    def tensor_of(pz):
        return y * ZH + pz // ZL

    def ahead(dx, dz, dc):
        return (x + dx) % X, (z + dz) % zs, (core + dc) % CORES

    def step_offset(i):
        n = i - (ZL - 1)
        later = (n + groups) // groups
        rest = later * (1 - (i + 1) // groups)
        j = rest * (n * later % (plane - 1) + 1)
        k = (1 - later) * (i + 1) + rest * (n * later // (plane - 1))
        far = (k % 2) * (ZL - 1 - k // 2) + (1 - k % 2) * (k // 2)
        return j // CORES, far, j % CORES

    def towards(i):
        dx, dz, dc = step_offset(i)
        return (((x + dx) % X) * ZL + (zl + dz) % ZL) * CORES + (core + dc) % CORES

    def source(i):
        dx, dz, dc = step_offset(i)
        return (((x + X - dx) % X) * ZL + (zl + ZL - dz) % ZL) * CORES + (core + CORES - dc) % CORES

    def cache_copy(c):
        return pltpu.make_async_copy(
            cache_ref.at[pl.ds(c * per, per)], cbuf.at[pl.ds(c * per, per)], cache_sem.at[c])

    staged = [
        pltpu.make_async_copy(src, dst, in_sem.at[n])
        for n, (src, dst) in enumerate(
            ((newq_ref, q_ref), (newkv_ref, fresh_ref), (perm_ref, perm_v), (plen_ref, plen_v)))
    ]
    for copy in staged[2:]:
        copy.start()
    for c in range(CHUNKS):
        cache_copy(c).start()
    for copy in staged[:2]:
        copy.start()

    barrier = pltpu.get_barrier_semaphore()

    def greet(sem, px, pz, pc):
        pl.semaphore_signal(
            sem, inc=1, device_id=(group_of(px, pz, pc), tensor_of(pz)), device_id_type=MESH)

    for k in range(1, ys):
        pl.semaphore_signal(barrier, inc=1, device_id=(g, ((y + k) % ys) * ZH + zh), device_id_type=MESH)
    for dz in range(1, zs):
        greet(barrier, *ahead(0, dz, 0))
    for j in range(1, plane):
        greet(barrier, *ahead(j // CORES, 0, j % CORES))

    staged[2].wait()
    staged[3].wait()
    square = (groups, rows)
    down = lax.broadcasted_iota(jnp.int32, square, 0)
    along = lax.broadcasted_iota(jnp.int32, square, 1)

    def column(ref):
        row = jnp.broadcast_to(ref[pl.ds(g, 1), :], square)
        return jnp.sum(jnp.where(down == along, row, 0), axis=1, keepdims=True)

    match = column(perm_v) == along
    position = jnp.sum(jnp.where(match, down, 0), axis=0, keepdims=True)
    length = jnp.sum(jnp.where(match, column(plen_v), 0), axis=0, keepdims=True)
    meta[0:1, 0:groups] = jnp.minimum(position, rows - 1)
    meta[1:2, 0:groups] = jnp.where(position < rows, length, 0)
    to_scalar = pltpu.make_async_copy(meta, where_ref, in_sem.at[2])
    to_scalar.start()

    size = tensors * tok
    r_out = lax.broadcasted_iota(jnp.int32, (size, size), 0)
    r_in = lax.broadcasted_iota(jnp.int32, (size, size), 1)
    pair = r_out // piece + y
    pair = jnp.where(pair >= ys, pair - ys, pair)
    wanted = (r_out % tok) * tensors + pair * ZH + (r_out % piece) // tok
    shuffle = jnp.where(wanted == r_in, 1.0, 0.0).astype(jnp.bfloat16)

    def kv_copy(k, c):
        return pltpu.make_async_remote_copy(
            src_ref=kvsend.at[k - 1, pl.ds(c * per, per)],
            dst_ref=kvrecv.at[pl.ds(c * per, per), y],
            send_sem=kv_send_sem.at[k - 1, c], recv_sem=kv_recv_sem.at[k - 1, c],
            device_id=(g, ((y + k) % ys) * ZH + zh), device_id_type=MESH)

    def regroup(c):
        def one(i, _):
            for u in range(2):
                r = c * per + i * 2 + u
                cache = cbuf[where_ref[0, source(r)]]
                moved = jnp.dot(shuffle, cache, preferred_element_type=jnp.float32).astype(jnp.bfloat16)
                kvrecv[r, y] = moved[:piece]
                for k in range(1, ys):
                    kvsend[k - 1, r] = moved[k * piece:(k + 1) * piece]
            return 0

        lax.fori_loop(0, per // 2, one, 0)

    def send_kv(c):
        for k in range(1, ys):
            kv_copy(k, c).start()

    def q_copy(peer, tensor):
        return pltpu.make_async_remote_copy(
            src_ref=q_ref.at[peer], dst_ref=qbuf.at[g, zh], send_sem=q_send_sem,
            recv_sem=q_recv_sem.at[g], device_id=(peer, tensor), device_id_type=MESH)

    def send_q(i, _):
        peer = towards(i)
        for h in range(ZH):
            q_copy(peer, y * ZH + h).start()
        return 0

    to_scalar.wait()
    for c in range(CHUNKS):
        cache_copy(c).wait()
    regroup(0)
    staged[0].wait()
    pltpu.make_async_copy(q_ref.at[g], qbuf.at[g, zh], q_recv_sem.at[g]).start()
    pl.semaphore_wait(barrier, ys - 1 + zs - 1 + plane - 1)
    for j in range(1, plane):
        greet(meet_sem, *ahead(j // CORES, 0, j % CORES))
    line = ZL - 1
    lax.fori_loop(0, line, send_q, 0)
    q_copy(g, y * ZH + 1 - zh).start()
    send_kv(0)
    regroup(1)
    send_kv(1)
    pl.semaphore_wait(meet_sem, plane - 1)
    done = line
    for c in range(2, CHUNKS):
        upto = line + (last - line) * (c - 1) // (CHUNKS - 2)
        lax.fori_loop(done, upto, send_q, 0)
        done = upto
        regroup(c)
        send_kv(c)
    lax.fori_loop(done, last, send_q, 0)

    staged[1].wait()
    at = per
    shape = (at, qn, steps)
    f_keep = lax.broadcasted_iota(jnp.int32, shape, 2) <= lax.broadcasted_iota(jnp.int32, shape, 1) // (qn // steps)

    def fresh_part(b, _):
        q = q_ref[pl.ds(b * at, at)]
        kv = fresh_ref[pl.ds(b * at, at)]
        s = jnp.einsum("bqd,bud->bqu", q, kv[:, :, :head], preferred_element_type=jnp.float32) * scale
        s = jnp.where(f_keep, s, NONE)
        m = jnp.max(s, axis=2, keepdims=True)
        p = jnp.exp(s - m)
        l = jnp.sum(p, axis=2, keepdims=True)
        o = jnp.einsum("bqu,bud->bqd", p.astype(jnp.bfloat16), kv[:, :, head:], preferred_element_type=jnp.float32)
        fo[pl.ds(b * at, at)] = o
        fm[pl.ds(b * at, at)] = jnp.broadcast_to(m, (at, qn, head))
        fl[pl.ds(b * at, at)] = jnp.broadcast_to(l, (at, qn, head))
        return 0

    lax.fori_loop(0, rows // at, fresh_part, 0)

    both = ZH * qn
    shape = (both, ys * piece)
    a_row = lax.broadcasted_iota(jnp.int32, shape, 0)
    a_col = lax.broadcasted_iota(jnp.int32, shape, 1)
    token = ((a_col // piece) * ZH + zh) * tok + a_col % tok
    token = jnp.where((a_col % piece) // tok == a_row // qn, token, 1 << 20)
    lane = lax.broadcasted_iota(jnp.int32, (both, 2 * qn), 1)
    diag = lax.broadcasted_iota(jnp.int32, (both, 2 * qn), 0) % qn
    on_m, on_l = lane == diag, lane == diag + qn

    def o_copy(peer, h):
        return pltpu.make_async_remote_copy(
            src_ref=osend.at[peer, h], dst_ref=orecv.at[g, zh], send_sem=o_send_sem,
            recv_sem=o_recv_sem.at[g], device_id=(peer, y * ZH + h), device_id_type=MESH)

    def s_copy(peer, h):
        return pltpu.make_async_remote_copy(
            src_ref=ssend.at[peer, h], dst_ref=srecv.at[g, zh], send_sem=s_send_sem,
            recv_sem=s_recv_sem.at[g], device_id=(peer, y * ZH + h), device_id_type=MESH)

    def attend(i):
        src = source(i)
        pltpu.make_async_copy(qbuf.at[src], qbuf.at[src], q_recv_sem.at[src]).wait()
        q = qbuf[src].reshape(both, head)
        kv = kvrecv[i].reshape(ys * piece, 2 * head)
        s = lax.dot_general(q, kv[:, :head], (((1,), (1,)), ((), ())), preferred_element_type=jnp.float32) * scale
        keep = token < where_ref[1, src]
        s = jnp.where(keep, s, NONE)
        m = jnp.max(s, axis=1, keepdims=True)
        p = jnp.where(keep, jnp.exp(s - m), 0.0)
        l = jnp.sum(p, axis=1, keepdims=True)
        o = jnp.dot(p.astype(jnp.bfloat16), kv[:, head:], preferred_element_type=jnp.float32)
        osend[src] = o.astype(jnp.bfloat16).reshape(ZH, qn, head)
        stat = jnp.where(on_m, m, jnp.where(on_l, l, 0.0))
        ssend[src] = jnp.sum(stat.reshape(ZH, qn, 2 * qn), axis=1, keepdims=True)
        return src

    def attend_send(i, _):
        src = attend(i)
        for h in range(ZH):
            s_copy(src, h).start()
            o_copy(src, h).start()
        return 0

    for c in range(CHUNKS):
        for k in range(1, ys):
            kv_copy(k, c).wait_recv()
        lax.fori_loop(c * per, min((c + 1) * per, last), attend_send, 0)
    attend(last)
    s_copy(g, 1 - zh).start()
    o_copy(g, 1 - zh).start()
    pltpu.make_async_copy(osend.at[g, zh], orecv.at[g, zh], o_recv_sem.at[g]).start()
    pltpu.make_async_copy(ssend.at[g, zh], srecv.at[g, zh], s_recv_sem.at[g]).start()

    c_lane = lax.broadcasted_iota(jnp.int32, (qn, 2 * qn), 1)
    c_row = lax.broadcasted_iota(jnp.int32, (qn, 2 * qn), 0)

    def combine(i, _):
        src = towards(i)
        pltpu.make_async_copy(srecv.at[src], srecv.at[src], s_recv_sem.at[src]).wait()
        pltpu.make_async_copy(orecv.at[src], orecv.at[src], o_recv_sem.at[src]).wait()
        m, l, o = [fm[src]], [fl[src]], [fo[src]]
        for h in range(ZH):
            stat = jnp.broadcast_to(srecv[src, h], (qn, 2 * qn))
            m.append(jnp.sum(jnp.where(c_lane == c_row, stat, 0.0), axis=1, keepdims=True))
            l.append(jnp.sum(jnp.where(c_lane == c_row + qn, stat, 0.0), axis=1, keepdims=True))
            o.append(orecv[src, h].astype(jnp.float32))
        top = functools.reduce(jnp.maximum, m)
        w = [jnp.exp(a - top) for a in m]
        den = sum(a * b for a, b in zip(w, l))
        num = sum(a * b for a, b in zip(w, o))
        out_ref[src] = (num / den).astype(jnp.bfloat16)
        return 0

    lax.fori_loop(0, groups, combine, 0)

    for c in range(CHUNKS):
        for k in range(1, ys):
            kv_copy(k, c).wait_send()
    for ref, sem in ((qbuf, q_send_sem), (osend, o_send_sem), (ssend, s_send_sem)):
        pltpu.make_async_copy(ref.at[pl.ds(0, last)], ref.at[pl.ds(0, last)], sem).wait()
        pltpu.make_async_copy(ref.at[last, 0], ref.at[last, 0], sem).wait()


def shards(cache_blocks, prompt_len, dest_perm, new_q, new_kv):
    groups = lax.axis_size("group")
    tensors = lax.axis_size("tensor")
    requests, _, tok, heads, width = cache_blocks.shape
    head = width // 2
    slots, steps, q_here = new_q.shape[1:4]
    qn = steps * q_here
    cache = cache_blocks.reshape(requests, tok * heads, width)
    queries = new_q.reshape(slots, qn, head)
    fresh = new_kv.reshape(slots, steps, width)
    ys = tensors // ZH
    piece = ZH * tok
    bf16, f32, i32 = jnp.bfloat16, jnp.float32, jnp.int32
    hbm = pl.BlockSpec(memory_space=pltpu.HBM)
    dma = pltpu.SemaphoreType.DMA
    out = pl.pallas_call(
        functools.partial(kernel, groups, tensors),
        out_shape=jax.ShapeDtypeStruct((slots, qn, head), bf16),
        in_specs=[hbm] * 5,
        out_specs=pl.BlockSpec(memory_space=pltpu.VMEM),
        scratch_shapes=[
            pltpu.VMEM((requests, tok * heads, width), bf16),
            pltpu.VMEM((slots, qn, head), bf16),
            pltpu.VMEM((slots, steps, width), bf16),
            pltpu.VMEM(dest_perm.shape, i32),
            pltpu.VMEM(prompt_len.shape, i32),
            pltpu.VMEM((8, 128), i32),
            pltpu.SMEM((8, 128), i32),
            pltpu.VMEM((ys - 1, requests, piece, width), bf16),
            pltpu.VMEM((requests, ys, piece, width), bf16),
            pltpu.VMEM((groups, ZH, qn, head), bf16),
            pltpu.VMEM((groups, ZH, qn, head), bf16),
            pltpu.VMEM((groups, ZH, qn, head), bf16),
            pltpu.VMEM((groups, ZH, 1, 2 * qn), f32),
            pltpu.VMEM((groups, ZH, 1, 2 * qn), f32),
            pltpu.VMEM((slots, qn, head), f32),
            pltpu.VMEM((slots, qn, head), f32),
            pltpu.VMEM((slots, qn, head), f32),
            dma((CHUNKS,)),
            dma((4,)),
            pltpu.SemaphoreType.REGULAR,
            dma((ys - 1, CHUNKS)),
            dma((ys - 1, CHUNKS)),
            dma,
            dma((groups,)),
            dma,
            dma((groups,)),
            dma,
            dma((groups,)),
        ],
        compiler_params=pltpu.CompilerParams(
            collective_id=0, has_side_effects=True, vmem_limit_bytes=48 << 20),
        cost_estimate=pl.CostEstimate(flops=1 << 30, bytes_accessed=12 << 20, transcendentals=1 << 20),
    )(*(pltpu.with_memory_space_constraint(a, pltpu.HBM) for a in (cache, dest_perm, prompt_len, queries, fresh)))
    return out.reshape(1, slots, steps, q_here, head)


def solution(mesh):
    placed = (
        P("group", None, "tensor", None, None),
        P(),
        P(),
        P("group", None, None, "tensor", None),
        P("group", None, None, "tensor", None),
    )
    return jax.shard_map(
        shards,
        mesh=mesh,
        in_specs=placed,
        out_specs=P("group", None, None, "tensor", None),
        check_vma=False,
    )
```

```python
import functools
import math

import jax
import jax.numpy as jnp
from jax import lax
from jax.experimental import pallas as pl
from jax.experimental.pallas import tpu as pltpu
from jax.sharding import PartitionSpec as P

MESH = pl.DeviceIdType.MESH

X, ZL, CORES = 4, 8, 2
ZH = 2
CHUNKS = 8
BEHIND = 3
NONE = -1e30


def kernel(groups, tensors, cache_ref, perm_ref, plen_ref, newq_ref, newkv_ref, out_ref,
           cbuf, q_ref, fresh_ref, perm_v, plen_v, meta, where_ref, kvsend, kvrecv, qbuf, osend, orecv, ssend, srecv, fo, fm, fl,
           cache_sem, in_sem, meet_sem, kv_send_sem, kv_recv_sem, q_send_sem, q_recv_sem,
           o_send_sem, o_recv_sem, s_send_sem, s_recv_sem):
    ys = tensors // ZH
    zs = ZH * ZL
    plane = X * CORES
    g = lax.axis_index("group")
    t = lax.axis_index("tensor")
    y, zh = t // ZH, t % ZH
    core, zl, x = g % CORES, (g // CORES) % ZL, g // (CORES * ZL)
    z = zh * ZL + zl
    rows, qn, head = q_ref.shape
    steps = fresh_ref.shape[1]
    tok = cache_ref.shape[1] // tensors
    piece = ZH * tok
    per = rows // CHUNKS
    scale = 1.0 / math.sqrt(head)
    last = groups - 1

    def group_of(px, pz, pc):
        return (px * ZL + pz % ZL) * CORES + pc

    def tensor_of(pz):
        return y * ZH + pz // ZL

    def ahead(dx, dz, dc):
        return (x + dx) % X, (z + dz) % zs, (core + dc) % CORES

    def step_offset(i):
        n = (i + 1) % groups
        j = n // ZL
        k = ZL - 1 - (n + j) % ZL
        far = ZL // 2 + (k // 2) * (1 - k % 2) - ((k + 1) // 2) * (k % 2)
        return j // CORES, far, j % CORES

    def towards(i):
        dx, dz, dc = step_offset(i)
        return (((x + dx) % X) * ZL + (zl + dz) % ZL) * CORES + (core + dc) % CORES

    def source(i):
        dx, dz, dc = step_offset(i)
        return (((x + X - dx) % X) * ZL + (zl + ZL - dz) % ZL) * CORES + (core + CORES - dc) % CORES

    def cache_copy(c):
        return pltpu.make_async_copy(
            cache_ref.at[pl.ds(c * per, per)], cbuf.at[pl.ds(c * per, per)], cache_sem.at[c])

    staged = [
        pltpu.make_async_copy(src, dst, in_sem.at[n])
        for n, (src, dst) in enumerate(
            ((newq_ref, q_ref), (newkv_ref, fresh_ref), (perm_ref, perm_v), (plen_ref, plen_v)))
    ]
    for copy in staged[2:] + staged[:1]:
        copy.start()
    for c in range(CHUNKS):
        cache_copy(c).start()
    staged[1].start()

    barrier = pltpu.get_barrier_semaphore()

    def greet(sem, px, pz, pc):
        pl.semaphore_signal(
            sem, inc=1, device_id=(group_of(px, pz, pc), tensor_of(pz)), device_id_type=MESH)

    for k in range(1, ys):
        pl.semaphore_signal(barrier, inc=1, device_id=(g, ((y + k) % ys) * ZH + zh), device_id_type=MESH)
    for dz in range(1, zs):
        greet(barrier, *ahead(0, dz, 0))
    for j in range(1, plane):
        greet(barrier, *ahead(j // CORES, 0, j % CORES))

    staged[2].wait()
    staged[3].wait()
    square = (groups, rows)
    down = lax.broadcasted_iota(jnp.int32, square, 0)
    along = lax.broadcasted_iota(jnp.int32, square, 1)

    def column(ref):
        row = jnp.broadcast_to(ref[pl.ds(g, 1), :], square)
        return jnp.sum(jnp.where(down == along, row, 0), axis=1, keepdims=True)

    match = column(perm_v) == along
    position = jnp.sum(jnp.where(match, down, 0), axis=0, keepdims=True)
    length = jnp.sum(jnp.where(match, column(plen_v), 0), axis=0, keepdims=True)
    meta[0:1, 0:groups] = jnp.minimum(position, rows - 1)
    meta[1:2, 0:groups] = jnp.where(position < rows, length, 0)
    to_scalar = pltpu.make_async_copy(meta, where_ref, in_sem.at[2])
    to_scalar.start()

    size = tensors * tok
    r_out = lax.broadcasted_iota(jnp.int32, (size, size), 0)
    r_in = lax.broadcasted_iota(jnp.int32, (size, size), 1)
    pair = r_out // piece + y
    pair = jnp.where(pair >= ys, pair - ys, pair)
    wanted = (r_out % tok) * tensors + pair * ZH + (r_out % piece) // tok
    shuffle = jnp.where(wanted == r_in, 1.0, 0.0).astype(jnp.bfloat16)

    def kv_copy(k, c):
        return pltpu.make_async_remote_copy(
            src_ref=kvsend.at[k - 1, pl.ds(c * per, per)],
            dst_ref=kvrecv.at[pl.ds(c * per, per), y],
            send_sem=kv_send_sem.at[k - 1, c], recv_sem=kv_recv_sem.at[k - 1, c],
            device_id=(g, ((y + k) % ys) * ZH + zh), device_id_type=MESH)

    def regroup(c):
        def one(i, _):
            for u in range(2):
                r = c * per + i * 2 + u
                cache = cbuf[where_ref[0, source(r)]]
                moved = jnp.dot(shuffle, cache, preferred_element_type=jnp.float32).astype(jnp.bfloat16)
                kvrecv[r, y] = moved[:piece]
                for k in range(1, ys):
                    kvsend[k - 1, r] = moved[k * piece:(k + 1) * piece]
            return 0

        lax.fori_loop(0, per // 2, one, 0)

    def send_kv(c):
        for k in range(1, ys):
            kv_copy(k, c).start()

    def q_copy(peer, tensor):
        return pltpu.make_async_remote_copy(
            src_ref=q_ref.at[peer], dst_ref=qbuf.at[g, zh], send_sem=q_send_sem,
            recv_sem=q_recv_sem.at[g], device_id=(peer, tensor), device_id_type=MESH)

    def send_q(i, _):
        peer = towards(i)
        for h in range(ZH):
            q_copy(peer, y * ZH + h).start()
        return 0

    staged[0].wait()
    pltpu.make_async_copy(q_ref.at[g], qbuf.at[g, zh], q_recv_sem.at[g]).start()
    pl.semaphore_wait(barrier, ys - 1 + zs - 1 + plane - 1)
    for j in range(1, plane):
        greet(meet_sem, *ahead(j // CORES, 0, j % CORES))
    line = ZL - 1
    lax.fori_loop(0, line, send_q, 0)
    q_copy(g, y * ZH + 1 - zh).start()
    to_scalar.wait()
    for c in range(CHUNKS):
        cache_copy(c).wait()
    for c in range(2):
        regroup(c)
        send_kv(c)
    pl.semaphore_wait(meet_sem, plane - 1)
    done = line
    for c in range(2, CHUNKS):
        upto = line + (last - line) * (c - 1) // (CHUNKS - 2)
        lax.fori_loop(done, upto, send_q, 0)
        done = upto
        regroup(c)
        send_kv(c)
    lax.fori_loop(done, last, send_q, 0)

    staged[1].wait()
    at = per
    shape = (at, qn, steps)
    f_keep = lax.broadcasted_iota(jnp.int32, shape, 2) <= lax.broadcasted_iota(jnp.int32, shape, 1) // (qn // steps)

    def fresh_part(b, _):
        q = q_ref[pl.ds(b * at, at)]
        kv = fresh_ref[pl.ds(b * at, at)]
        s = jnp.einsum("bqd,bud->bqu", q, kv[:, :, :head], preferred_element_type=jnp.float32) * scale
        s = jnp.where(f_keep, s, NONE)
        m = jnp.max(s, axis=2, keepdims=True)
        p = jnp.exp(s - m)
        l = jnp.sum(p, axis=2, keepdims=True)
        o = jnp.einsum("bqu,bud->bqd", p.astype(jnp.bfloat16), kv[:, :, head:], preferred_element_type=jnp.float32)
        fo[pl.ds(b * at, at)] = o
        fm[pl.ds(b * at, at)] = jnp.broadcast_to(m, (at, qn, head))
        fl[pl.ds(b * at, at)] = jnp.broadcast_to(l, (at, qn, head))
        return 0

    lax.fori_loop(0, rows // at, fresh_part, 0)

    both = ZH * qn
    shape = (both, ys * piece)
    a_row = lax.broadcasted_iota(jnp.int32, shape, 0)
    a_col = lax.broadcasted_iota(jnp.int32, shape, 1)
    token = ((a_col // piece) * ZH + zh) * tok + a_col % tok
    token = jnp.where((a_col % piece) // tok == a_row // qn, token, 1 << 20)
    lane = lax.broadcasted_iota(jnp.int32, (both, 2 * qn), 1)
    diag = lax.broadcasted_iota(jnp.int32, (both, 2 * qn), 0) % qn
    on_m, on_l = lane == diag, lane == diag + qn

    def o_copy(peer, h):
        return pltpu.make_async_remote_copy(
            src_ref=osend.at[peer, h], dst_ref=orecv.at[g, zh], send_sem=o_send_sem,
            recv_sem=o_recv_sem.at[g], device_id=(peer, y * ZH + h), device_id_type=MESH)

    def s_copy(peer, h):
        return pltpu.make_async_remote_copy(
            src_ref=ssend.at[peer, h], dst_ref=srecv.at[g, zh], send_sem=s_send_sem,
            recv_sem=s_recv_sem.at[g], device_id=(peer, y * ZH + h), device_id_type=MESH)

    def attend(i):
        src = source(i)
        pltpu.make_async_copy(qbuf.at[src], qbuf.at[src], q_recv_sem.at[src]).wait()
        q = qbuf[src].reshape(both, head)
        kv = kvrecv[i].reshape(ys * piece, 2 * head)
        s = lax.dot_general(q, kv[:, :head], (((1,), (1,)), ((), ())), preferred_element_type=jnp.float32) * scale
        keep = token < where_ref[1, src]
        s = jnp.where(keep, s, NONE)
        m = jnp.max(s, axis=1, keepdims=True)
        p = jnp.where(keep, jnp.exp(s - m), 0.0)
        l = jnp.sum(p, axis=1, keepdims=True)
        o = jnp.dot(p.astype(jnp.bfloat16), kv[:, head:], preferred_element_type=jnp.float32)
        osend[src] = o.astype(jnp.bfloat16).reshape(ZH, qn, head)
        stat = jnp.where(on_m, m, jnp.where(on_l, l, 0.0))
        ssend[src] = jnp.sum(stat.reshape(ZH, qn, 2 * qn), axis=1, keepdims=True)
        return src

    def attend_send(i, _):
        src = attend(i)
        for h in range(ZH):
            s_copy(src, h).start()
            o_copy(src, h).start()
        return 0

    arrived = 0
    for c in range(CHUNKS):
        while arrived < min(c + 1 + BEHIND, CHUNKS):
            for k in range(1, ys):
                kv_copy(k, arrived).wait_recv()
            arrived += 1
        lax.fori_loop(c * per, min((c + 1) * per, last), attend_send, 0)
    attend(last)
    s_copy(g, 1 - zh).start()
    o_copy(g, 1 - zh).start()
    pltpu.make_async_copy(osend.at[g, zh], orecv.at[g, zh], o_recv_sem.at[g]).start()
    pltpu.make_async_copy(ssend.at[g, zh], srecv.at[g, zh], s_recv_sem.at[g]).start()

    c_lane = lax.broadcasted_iota(jnp.int32, (qn, 2 * qn), 1)
    c_row = lax.broadcasted_iota(jnp.int32, (qn, 2 * qn), 0)

    def combine(i, _):
        src = towards(i)
        pltpu.make_async_copy(srecv.at[src], srecv.at[src], s_recv_sem.at[src]).wait()
        pltpu.make_async_copy(orecv.at[src], orecv.at[src], o_recv_sem.at[src]).wait()
        m, l, o = [fm[src]], [fl[src]], [fo[src]]
        for h in range(ZH):
            stat = jnp.broadcast_to(srecv[src, h], (qn, 2 * qn))
            m.append(jnp.sum(jnp.where(c_lane == c_row, stat, 0.0), axis=1, keepdims=True))
            l.append(jnp.sum(jnp.where(c_lane == c_row + qn, stat, 0.0), axis=1, keepdims=True))
            o.append(orecv[src, h].astype(jnp.float32))
        top = functools.reduce(jnp.maximum, m)
        w = [jnp.exp(a - top) for a in m]
        den = sum(a * b for a, b in zip(w, l))
        num = sum(a * b for a, b in zip(w, o))
        out_ref[src] = (num / den).astype(jnp.bfloat16)
        return 0

    lax.fori_loop(0, groups, combine, 0)

    for c in range(CHUNKS):
        for k in range(1, ys):
            kv_copy(k, c).wait_send()
    for ref, sem in ((qbuf, q_send_sem), (osend, o_send_sem), (ssend, s_send_sem)):
        pltpu.make_async_copy(ref.at[pl.ds(0, last)], ref.at[pl.ds(0, last)], sem).wait()
        pltpu.make_async_copy(ref.at[last, 0], ref.at[last, 0], sem).wait()


def shards(cache_blocks, prompt_len, dest_perm, new_q, new_kv):
    groups = lax.axis_size("group")
    tensors = lax.axis_size("tensor")
    requests, _, tok, heads, width = cache_blocks.shape
    head = width // 2
    slots, steps, q_here = new_q.shape[1:4]
    qn = steps * q_here
    cache = cache_blocks.reshape(requests, tok * heads, width)
    queries = new_q.reshape(slots, qn, head)
    fresh = new_kv.reshape(slots, steps, width)
    ys = tensors // ZH
    piece = ZH * tok
    bf16, f32, i32 = jnp.bfloat16, jnp.float32, jnp.int32
    hbm = pl.BlockSpec(memory_space=pltpu.HBM)
    dma = pltpu.SemaphoreType.DMA
    out = pl.pallas_call(
        functools.partial(kernel, groups, tensors),
        out_shape=jax.ShapeDtypeStruct((slots, qn, head), bf16),
        in_specs=[hbm] * 5,
        out_specs=pl.BlockSpec(memory_space=pltpu.VMEM),
        scratch_shapes=[
            pltpu.VMEM((requests, tok * heads, width), bf16),
            pltpu.VMEM((slots, qn, head), bf16),
            pltpu.VMEM((slots, steps, width), bf16),
            pltpu.VMEM(dest_perm.shape, i32),
            pltpu.VMEM(prompt_len.shape, i32),
            pltpu.VMEM((8, 128), i32),
            pltpu.SMEM((8, 128), i32),
            pltpu.VMEM((ys - 1, requests, piece, width), bf16),
            pltpu.VMEM((requests, ys, piece, width), bf16),
            pltpu.VMEM((groups, ZH, qn, head), bf16),
            pltpu.VMEM((groups, ZH, qn, head), bf16),
            pltpu.VMEM((groups, ZH, qn, head), bf16),
            pltpu.VMEM((groups, ZH, 1, 2 * qn), f32),
            pltpu.VMEM((groups, ZH, 1, 2 * qn), f32),
            pltpu.VMEM((slots, qn, head), f32),
            pltpu.VMEM((slots, qn, head), f32),
            pltpu.VMEM((slots, qn, head), f32),
            dma((CHUNKS,)),
            dma((4,)),
            pltpu.SemaphoreType.REGULAR,
            dma((ys - 1, CHUNKS)),
            dma((ys - 1, CHUNKS)),
            dma,
            dma((groups,)),
            dma,
            dma((groups,)),
            dma,
            dma((groups,)),
        ],
        compiler_params=pltpu.CompilerParams(
            collective_id=0, has_side_effects=True, vmem_limit_bytes=48 << 20),
        cost_estimate=pl.CostEstimate(flops=1 << 30, bytes_accessed=12 << 20, transcendentals=1 << 20),
    )(*(pltpu.with_memory_space_constraint(a, pltpu.HBM) for a in (cache, dest_perm, prompt_len, queries, fresh)))
    return out.reshape(1, slots, steps, q_here, head)


def solution(mesh):
    placed = (
        P("group", None, "tensor", None, None),
        P(),
        P(),
        P("group", None, None, "tensor", None),
        P("group", None, None, "tensor", None),
    )
    return jax.shard_map(
        shards,
        mesh=mesh,
        in_specs=placed,
        out_specs=P("group", None, None, "tensor", None),
        check_vma=False,
    )
```

```python
import functools
import math

import jax
import jax.numpy as jnp
from jax import lax
from jax.experimental import pallas as pl
from jax.experimental.pallas import tpu as pltpu
from jax.sharding import PartitionSpec as P

MESH = pl.DeviceIdType.MESH

X, ZL, CORES = 4, 8, 2
ZH = 2
CHUNKS = 8
BEHIND = 3
NONE = -1e30


def kernel(groups, tensors, cache_ref, perm_ref, plen_ref, newq_ref, newkv_ref, out_ref,
           cbuf, q_ref, fresh_ref, perm_v, plen_v, meta, where_ref, kvsend, kvrecv, qbuf, osend, orecv, ssend, srecv, fo, fm, fl,
           cache_sem, in_sem, meet_sem, kv_send_sem, kv_recv_sem, q_send_sem, q_recv_sem,
           o_send_sem, o_recv_sem, s_send_sem, s_recv_sem):
    ys = tensors // ZH
    zs = ZH * ZL
    plane = X * CORES
    g = lax.axis_index("group")
    t = lax.axis_index("tensor")
    y, zh = t // ZH, t % ZH
    core, zl, x = g % CORES, (g // CORES) % ZL, g // (CORES * ZL)
    z = zh * ZL + zl
    rows, qn, head = q_ref.shape
    steps = fresh_ref.shape[1]
    tok = cache_ref.shape[1] // tensors
    piece = ZH * tok
    per = rows // CHUNKS
    scale = 1.0 / math.sqrt(head)
    last = groups - 1

    def group_of(px, pz, pc):
        return (px * ZL + pz % ZL) * CORES + pc

    def tensor_of(pz):
        return y * ZH + pz // ZL

    def ahead(dx, dz, dc):
        return (x + dx) % X, (z + dz) % zs, (core + dc) % CORES

    def step_offset(i):
        n = (i + 1) % groups
        j = n // ZL
        k = ZL - 1 - (n + j) % ZL
        far = ZL // 2 + (k // 2) * (1 - k % 2) - ((k + 1) // 2) * (k % 2)
        return j // CORES, far, j % CORES

    def towards(i):
        dx, dz, dc = step_offset(i)
        return (((x + dx) % X) * ZL + (zl + dz) % ZL) * CORES + (core + dc) % CORES

    def source(i):
        dx, dz, dc = step_offset(i)
        return (((x + X - dx) % X) * ZL + (zl + ZL - dz) % ZL) * CORES + (core + CORES - dc) % CORES

    def cache_copy(c):
        return pltpu.make_async_copy(
            cache_ref.at[pl.ds(c * per, per)], cbuf.at[pl.ds(c * per, per)], cache_sem.at[c])

    staged = [
        pltpu.make_async_copy(src, dst, in_sem.at[n])
        for n, (src, dst) in enumerate(
            ((newq_ref, q_ref), (newkv_ref, fresh_ref), (perm_ref, perm_v), (plen_ref, plen_v)))
    ]
    for copy in staged[2:] + staged[:1]:
        copy.start()
    for c in range(CHUNKS):
        cache_copy(c).start()
    staged[1].start()

    barrier = pltpu.get_barrier_semaphore()

    def greet(sem, px, pz, pc):
        pl.semaphore_signal(
            sem, inc=1, device_id=(group_of(px, pz, pc), tensor_of(pz)), device_id_type=MESH)

    for k in range(1, ys):
        pl.semaphore_signal(barrier, inc=1, device_id=(g, ((y + k) % ys) * ZH + zh), device_id_type=MESH)
    for dz in range(1, zs):
        greet(barrier, *ahead(0, dz, 0))
    for j in range(1, plane):
        greet(barrier, *ahead(j // CORES, 0, j % CORES))

    staged[2].wait()
    staged[3].wait()
    square = (groups, rows)
    down = lax.broadcasted_iota(jnp.int32, square, 0)
    along = lax.broadcasted_iota(jnp.int32, square, 1)

    def column(ref):
        row = jnp.broadcast_to(ref[pl.ds(g, 1), :], square)
        return jnp.sum(jnp.where(down == along, row, 0), axis=1, keepdims=True)

    match = column(perm_v) == along
    position = jnp.sum(jnp.where(match, down, 0), axis=0, keepdims=True)
    length = jnp.sum(jnp.where(match, column(plen_v), 0), axis=0, keepdims=True)
    meta[0:1, 0:groups] = jnp.minimum(position, rows - 1)
    meta[1:2, 0:groups] = jnp.where(position < rows, length, 0)
    to_scalar = pltpu.make_async_copy(meta, where_ref, in_sem.at[2])
    to_scalar.start()

    size = tensors * tok
    r_out = lax.broadcasted_iota(jnp.int32, (size, size), 0)
    r_in = lax.broadcasted_iota(jnp.int32, (size, size), 1)
    pair = r_out // piece + y
    pair = jnp.where(pair >= ys, pair - ys, pair)
    wanted = (r_out % tok) * tensors + pair * ZH + (r_out % piece) // tok
    shuffle = jnp.where(wanted == r_in, 1.0, 0.0).astype(jnp.bfloat16)

    def kv_copy(k, c):
        return pltpu.make_async_remote_copy(
            src_ref=kvsend.at[k - 1, pl.ds(c * per, per)],
            dst_ref=kvrecv.at[pl.ds(c * per, per), y],
            send_sem=kv_send_sem.at[k - 1, c], recv_sem=kv_recv_sem.at[k - 1, c],
            device_id=(g, ((y + k) % ys) * ZH + zh), device_id_type=MESH)

    def regroup(c):
        def one(i, _):
            for u in range(2):
                r = c * per + i * 2 + u
                cache = cbuf[where_ref[0, source(r)]]
                moved = jnp.dot(shuffle, cache, preferred_element_type=jnp.float32).astype(jnp.bfloat16)
                kvrecv[r, y] = moved[:piece]
                for k in range(1, ys):
                    kvsend[k - 1, r] = moved[k * piece:(k + 1) * piece]
            return 0

        lax.fori_loop(0, per // 2, one, 0)

    def send_kv(c):
        for k in range(1, ys):
            kv_copy(k, c).start()

    def q_copy(peer, tensor):
        return pltpu.make_async_remote_copy(
            src_ref=q_ref.at[peer], dst_ref=qbuf.at[g, zh], send_sem=q_send_sem,
            recv_sem=q_recv_sem.at[g], device_id=(peer, tensor), device_id_type=MESH)

    def send_q(i, _):
        peer = towards(i)
        for h in range(ZH):
            q_copy(peer, y * ZH + h).start()
        return 0

    staged[0].wait()
    pltpu.make_async_copy(q_ref.at[g], qbuf.at[g, zh], q_recv_sem.at[g]).start()
    pl.semaphore_wait(barrier, ys - 1 + zs - 1 + plane - 1)
    for j in range(1, plane):
        greet(meet_sem.at[j], *ahead(j // CORES, 0, j % CORES))
    line = ZL - 1
    lax.fori_loop(0, line, send_q, 0)
    q_copy(g, y * ZH + 1 - zh).start()
    to_scalar.wait()
    for c in range(CHUNKS):
        cache_copy(c).wait()
    regroup(0)
    send_kv(0)
    for c in range(1, max(CHUNKS, plane)):
        if c < plane:
            back = (X - c // CORES) % X * CORES + (CORES - c % CORES) % CORES
            pl.semaphore_wait(meet_sem.at[back], 1)
            lax.fori_loop(line + (c - 1) * ZL, line + c * ZL, send_q, 0)
        if c < CHUNKS:
            regroup(c)
            send_kv(c)

    staged[1].wait()
    at = per
    shape = (at, qn, steps)
    f_keep = lax.broadcasted_iota(jnp.int32, shape, 2) <= lax.broadcasted_iota(jnp.int32, shape, 1) // (qn // steps)

    def fresh_part(b, _):
        q = q_ref[pl.ds(b * at, at)]
        kv = fresh_ref[pl.ds(b * at, at)]
        s = jnp.einsum("bqd,bud->bqu", q, kv[:, :, :head], preferred_element_type=jnp.float32) * scale
        s = jnp.where(f_keep, s, NONE)
        m = jnp.max(s, axis=2, keepdims=True)
        p = jnp.exp(s - m)
        l = jnp.sum(p, axis=2, keepdims=True)
        o = jnp.einsum("bqu,bud->bqd", p.astype(jnp.bfloat16), kv[:, :, head:], preferred_element_type=jnp.float32)
        fo[pl.ds(b * at, at)] = o
        fm[pl.ds(b * at, at)] = jnp.broadcast_to(m, (at, qn, head))
        fl[pl.ds(b * at, at)] = jnp.broadcast_to(l, (at, qn, head))
        return 0

    lax.fori_loop(0, rows // at, fresh_part, 0)

    both = ZH * qn
    shape = (both, ys * piece)
    a_row = lax.broadcasted_iota(jnp.int32, shape, 0)
    a_col = lax.broadcasted_iota(jnp.int32, shape, 1)
    token = ((a_col // piece) * ZH + zh) * tok + a_col % tok
    token = jnp.where((a_col % piece) // tok == a_row // qn, token, 1 << 20)
    lane = lax.broadcasted_iota(jnp.int32, (both, 2 * qn), 1)
    diag = lax.broadcasted_iota(jnp.int32, (both, 2 * qn), 0) % qn
    on_m, on_l = lane == diag, lane == diag + qn

    def o_copy(peer, h):
        return pltpu.make_async_remote_copy(
            src_ref=osend.at[peer, h], dst_ref=orecv.at[g, zh], send_sem=o_send_sem,
            recv_sem=o_recv_sem.at[g], device_id=(peer, y * ZH + h), device_id_type=MESH)

    def s_copy(peer, h):
        return pltpu.make_async_remote_copy(
            src_ref=ssend.at[peer, h], dst_ref=srecv.at[g, zh], send_sem=s_send_sem,
            recv_sem=s_recv_sem.at[g], device_id=(peer, y * ZH + h), device_id_type=MESH)

    def attend(i):
        src = source(i)
        pltpu.make_async_copy(qbuf.at[src], qbuf.at[src], q_recv_sem.at[src]).wait()
        q = qbuf[src].reshape(both, head)
        kv = kvrecv[i].reshape(ys * piece, 2 * head)
        s = lax.dot_general(q, kv[:, :head], (((1,), (1,)), ((), ())), preferred_element_type=jnp.float32) * scale
        keep = token < where_ref[1, src]
        s = jnp.where(keep, s, NONE)
        m = jnp.max(s, axis=1, keepdims=True)
        p = jnp.where(keep, jnp.exp(s - m), 0.0)
        l = jnp.sum(p, axis=1, keepdims=True)
        o = jnp.dot(p.astype(jnp.bfloat16), kv[:, head:], preferred_element_type=jnp.float32)
        osend[src] = o.astype(jnp.bfloat16).reshape(ZH, qn, head)
        stat = jnp.where(on_m, m, jnp.where(on_l, l, 0.0))
        ssend[src] = jnp.sum(stat.reshape(ZH, qn, 2 * qn), axis=1, keepdims=True)
        return src

    def attend_send(i, _):
        src = attend(i)
        for h in range(ZH):
            s_copy(src, h).start()
            o_copy(src, h).start()
        return 0

    arrived = 0
    for c in range(CHUNKS):
        while arrived < min(c + 1 + BEHIND, CHUNKS):
            for k in range(1, ys):
                kv_copy(k, arrived).wait_recv()
            arrived += 1
        lax.fori_loop(c * per, min((c + 1) * per, last), attend_send, 0)
    attend(last)
    s_copy(g, 1 - zh).start()
    o_copy(g, 1 - zh).start()
    pltpu.make_async_copy(osend.at[g, zh], orecv.at[g, zh], o_recv_sem.at[g]).start()
    pltpu.make_async_copy(ssend.at[g, zh], srecv.at[g, zh], s_recv_sem.at[g]).start()

    c_lane = lax.broadcasted_iota(jnp.int32, (qn, 2 * qn), 1)
    c_row = lax.broadcasted_iota(jnp.int32, (qn, 2 * qn), 0)

    def combine(i, _):
        src = towards(i)
        pltpu.make_async_copy(srecv.at[src], srecv.at[src], s_recv_sem.at[src]).wait()
        pltpu.make_async_copy(orecv.at[src], orecv.at[src], o_recv_sem.at[src]).wait()
        m, l, o = [fm[src]], [fl[src]], [fo[src]]
        for h in range(ZH):
            stat = jnp.broadcast_to(srecv[src, h], (qn, 2 * qn))
            m.append(jnp.sum(jnp.where(c_lane == c_row, stat, 0.0), axis=1, keepdims=True))
            l.append(jnp.sum(jnp.where(c_lane == c_row + qn, stat, 0.0), axis=1, keepdims=True))
            o.append(orecv[src, h].astype(jnp.float32))
        top = functools.reduce(jnp.maximum, m)
        w = [jnp.exp(a - top) for a in m]
        den = sum(a * b for a, b in zip(w, l))
        num = sum(a * b for a, b in zip(w, o))
        out_ref[src] = (num / den).astype(jnp.bfloat16)
        return 0

    lax.fori_loop(0, groups, combine, 0)

    for c in range(CHUNKS):
        for k in range(1, ys):
            kv_copy(k, c).wait_send()
    for ref, sem in ((qbuf, q_send_sem), (osend, o_send_sem), (ssend, s_send_sem)):
        pltpu.make_async_copy(ref.at[pl.ds(0, last)], ref.at[pl.ds(0, last)], sem).wait()
        pltpu.make_async_copy(ref.at[last, 0], ref.at[last, 0], sem).wait()


def shards(cache_blocks, prompt_len, dest_perm, new_q, new_kv):
    groups = lax.axis_size("group")
    tensors = lax.axis_size("tensor")
    requests, _, tok, heads, width = cache_blocks.shape
    head = width // 2
    slots, steps, q_here = new_q.shape[1:4]
    qn = steps * q_here
    cache = cache_blocks.reshape(requests, tok * heads, width)
    queries = new_q.reshape(slots, qn, head)
    fresh = new_kv.reshape(slots, steps, width)
    ys = tensors // ZH
    piece = ZH * tok
    bf16, f32, i32 = jnp.bfloat16, jnp.float32, jnp.int32
    hbm = pl.BlockSpec(memory_space=pltpu.HBM)
    dma = pltpu.SemaphoreType.DMA
    out = pl.pallas_call(
        functools.partial(kernel, groups, tensors),
        out_shape=jax.ShapeDtypeStruct((slots, qn, head), bf16),
        in_specs=[hbm] * 5,
        out_specs=pl.BlockSpec(memory_space=pltpu.VMEM),
        scratch_shapes=[
            pltpu.VMEM((requests, tok * heads, width), bf16),
            pltpu.VMEM((slots, qn, head), bf16),
            pltpu.VMEM((slots, steps, width), bf16),
            pltpu.VMEM(dest_perm.shape, i32),
            pltpu.VMEM(prompt_len.shape, i32),
            pltpu.VMEM((8, 128), i32),
            pltpu.SMEM((8, 128), i32),
            pltpu.VMEM((ys - 1, requests, piece, width), bf16),
            pltpu.VMEM((requests, ys, piece, width), bf16),
            pltpu.VMEM((groups, ZH, qn, head), bf16),
            pltpu.VMEM((groups, ZH, qn, head), bf16),
            pltpu.VMEM((groups, ZH, qn, head), bf16),
            pltpu.VMEM((groups, ZH, 1, 2 * qn), f32),
            pltpu.VMEM((groups, ZH, 1, 2 * qn), f32),
            pltpu.VMEM((slots, qn, head), f32),
            pltpu.VMEM((slots, qn, head), f32),
            pltpu.VMEM((slots, qn, head), f32),
            dma((CHUNKS,)),
            dma((4,)),
            pltpu.SemaphoreType.REGULAR((X * CORES,)),
            dma((ys - 1, CHUNKS)),
            dma((ys - 1, CHUNKS)),
            dma,
            dma((groups,)),
            dma,
            dma((groups,)),
            dma,
            dma((groups,)),
        ],
        compiler_params=pltpu.CompilerParams(
            collective_id=0, has_side_effects=True, vmem_limit_bytes=48 << 20),
        cost_estimate=pl.CostEstimate(flops=1 << 30, bytes_accessed=12 << 20, transcendentals=1 << 20),
    )(*(pltpu.with_memory_space_constraint(a, pltpu.HBM) for a in (cache, dest_perm, prompt_len, queries, fresh)))
    return out.reshape(1, slots, steps, q_here, head)


def solution(mesh):
    placed = (
        P("group", None, "tensor", None, None),
        P(),
        P(),
        P("group", None, None, "tensor", None),
        P("group", None, None, "tensor", None),
    )
    return jax.shard_map(
        shards,
        mesh=mesh,
        in_specs=placed,
        out_specs=P("group", None, None, "tensor", None),
        check_vma=False,
    )
```

```python
import functools
import math

import jax
import jax.numpy as jnp
from jax import lax
from jax.experimental import pallas as pl
from jax.experimental.pallas import tpu as pltpu
from jax.sharding import PartitionSpec as P

MESH = pl.DeviceIdType.MESH

X, ZL, CORES = 4, 8, 2
ZH = 2
CHUNKS = 8
BEHIND = 3
NONE = -1e30


def kernel(groups, tensors, cache_ref, perm_ref, plen_ref, newq_ref, newkv_ref, out_ref,
           cbuf, q_ref, fresh_ref, perm_v, plen_v, meta, where_ref, kvsend, kvrecv, qbuf, osend, orecv, ssend, srecv, fo, fm, fl,
           cache_sem, in_sem, meet_sem, kv_send_sem, kv_recv_sem, q_send_sem, q_recv_sem,
           o_send_sem, o_recv_sem, s_send_sem, s_recv_sem):
    ys = tensors // ZH
    zs = ZH * ZL
    plane = X * CORES
    g = lax.axis_index("group")
    t = lax.axis_index("tensor")
    y, zh = t // ZH, t % ZH
    core, zl, x = g % CORES, (g // CORES) % ZL, g // (CORES * ZL)
    z = zh * ZL + zl
    rows, qn, head = q_ref.shape
    steps = fresh_ref.shape[1]
    tok = cache_ref.shape[1] // tensors
    piece = ZH * tok
    per = rows // CHUNKS
    scale = 1.0 / math.sqrt(head)
    last = groups - 1

    def group_of(px, pz, pc):
        return (px * ZL + pz % ZL) * CORES + pc

    def tensor_of(pz):
        return y * ZH + pz // ZL

    def ahead(dx, dz, dc):
        return (x + dx) % X, (z + dz) % zs, (core + dc) % CORES

    def step_offset(i):
        n = (i + 1) % groups
        j = n // ZL
        k = ZL - 1 - (n + j) % ZL
        far = ZL // 2 + (k // 2) * (1 - k % 2) - ((k + 1) // 2) * (k % 2)
        return j // CORES, far, j % CORES

    def towards(i):
        dx, dz, dc = step_offset(i)
        return (((x + dx) % X) * ZL + (zl + dz) % ZL) * CORES + (core + dc) % CORES

    def source(i):
        dx, dz, dc = step_offset(i)
        return (((x + X - dx) % X) * ZL + (zl + ZL - dz) % ZL) * CORES + (core + CORES - dc) % CORES

    def cache_copy(c):
        return pltpu.make_async_copy(
            cache_ref.at[pl.ds(c * per, per)], cbuf.at[pl.ds(c * per, per)], cache_sem.at[c])

    staged = [
        pltpu.make_async_copy(src, dst, in_sem.at[n])
        for n, (src, dst) in enumerate(
            ((newq_ref, q_ref), (newkv_ref, fresh_ref), (perm_ref, perm_v), (plen_ref, plen_v)))
    ]
    for copy in staged[2:] + staged[:1]:
        copy.start()
    for c in range(CHUNKS):
        cache_copy(c).start()
    staged[1].start()

    barrier = pltpu.get_barrier_semaphore()

    def greet(sem, px, pz, pc):
        pl.semaphore_signal(
            sem, inc=1, device_id=(group_of(px, pz, pc), tensor_of(pz)), device_id_type=MESH)

    for k in range(1, ys):
        pl.semaphore_signal(barrier, inc=1, device_id=(g, ((y + k) % ys) * ZH + zh), device_id_type=MESH)
    for dz in range(1, zs):
        greet(barrier, *ahead(0, dz, 0))
    for j in range(1, plane):
        greet(barrier, *ahead(j // CORES, 0, j % CORES))

    staged[2].wait()
    staged[3].wait()
    square = (groups, rows)
    down = lax.broadcasted_iota(jnp.int32, square, 0)
    along = lax.broadcasted_iota(jnp.int32, square, 1)

    def column(ref):
        row = jnp.broadcast_to(ref[pl.ds(g, 1), :], square)
        return jnp.sum(jnp.where(down == along, row, 0), axis=1, keepdims=True)

    match = column(perm_v) == along
    position = jnp.sum(jnp.where(match, down, 0), axis=0, keepdims=True)
    length = jnp.sum(jnp.where(match, column(plen_v), 0), axis=0, keepdims=True)
    meta[0:1, 0:groups] = jnp.minimum(position, rows - 1)
    meta[1:2, 0:groups] = jnp.where(position < rows, length, 0)
    to_scalar = pltpu.make_async_copy(meta, where_ref, in_sem.at[2])
    to_scalar.start()

    size = tensors * tok
    r_out = lax.broadcasted_iota(jnp.int32, (size, size), 0)
    r_in = lax.broadcasted_iota(jnp.int32, (size, size), 1)
    pair = r_out // piece + y
    pair = jnp.where(pair >= ys, pair - ys, pair)
    wanted = (r_out % tok) * tensors + pair * ZH + (r_out % piece) // tok
    shuffle = jnp.where(wanted == r_in, 1.0, 0.0).astype(jnp.bfloat16)

    def kv_copy(k, c):
        return pltpu.make_async_remote_copy(
            src_ref=kvsend.at[k - 1, pl.ds(c * per, per)],
            dst_ref=kvrecv.at[pl.ds(c * per, per), y],
            send_sem=kv_send_sem.at[k - 1, c], recv_sem=kv_recv_sem.at[k - 1, c],
            device_id=(g, ((y + k) % ys) * ZH + zh), device_id_type=MESH)

    def regroup(c):
        def one(i, _):
            for u in range(2):
                r = c * per + i * 2 + u
                cache = cbuf[where_ref[0, source(r)]]
                moved = jnp.dot(shuffle, cache, preferred_element_type=jnp.float32).astype(jnp.bfloat16)
                kvrecv[r, y] = moved[:piece]
                for k in range(1, ys):
                    kvsend[k - 1, r] = moved[k * piece:(k + 1) * piece]
            return 0

        lax.fori_loop(0, per // 2, one, 0)

    def send_kv(c):
        for k in range(1, ys):
            kv_copy(k, c).start()

    def q_copy(peer, tensor):
        return pltpu.make_async_remote_copy(
            src_ref=q_ref.at[peer], dst_ref=qbuf.at[g, zh], send_sem=q_send_sem,
            recv_sem=q_recv_sem.at[g], device_id=(peer, tensor), device_id_type=MESH)

    def send_q(i, _):
        peer = towards(i)
        for h in range(ZH):
            q_copy(peer, y * ZH + (zh + 1 + h) % ZH).start()
        return 0

    staged[0].wait()
    pltpu.make_async_copy(q_ref.at[g], qbuf.at[g, zh], q_recv_sem.at[g]).start()
    pl.semaphore_wait(barrier, ys - 1 + zs - 1 + plane - 1)
    for j in range(1, plane):
        greet(meet_sem, *ahead(j // CORES, 0, j % CORES))
    line = ZL - 1
    lax.fori_loop(0, line, send_q, 0)
    q_copy(g, y * ZH + 1 - zh).start()
    to_scalar.wait()
    for c in range(CHUNKS):
        cache_copy(c).wait()
    for c in range(2):
        regroup(c)
        send_kv(c)
    pl.semaphore_wait(meet_sem, plane - 1)
    done = line
    for c in range(2, CHUNKS):
        upto = line + (last - line) * (c - 1) // (CHUNKS - 2)
        lax.fori_loop(done, upto, send_q, 0)
        done = upto
        regroup(c)
        send_kv(c)
    lax.fori_loop(done, last, send_q, 0)

    staged[1].wait()
    at = per
    shape = (at, qn, steps)
    f_keep = lax.broadcasted_iota(jnp.int32, shape, 2) <= lax.broadcasted_iota(jnp.int32, shape, 1) // (qn // steps)

    def fresh_part(b, _):
        q = q_ref[pl.ds(b * at, at)]
        kv = fresh_ref[pl.ds(b * at, at)]
        s = jnp.einsum("bqd,bud->bqu", q, kv[:, :, :head], preferred_element_type=jnp.float32) * scale
        s = jnp.where(f_keep, s, NONE)
        m = jnp.max(s, axis=2, keepdims=True)
        p = jnp.exp(s - m)
        l = jnp.sum(p, axis=2, keepdims=True)
        o = jnp.einsum("bqu,bud->bqd", p.astype(jnp.bfloat16), kv[:, :, head:], preferred_element_type=jnp.float32)
        fo[pl.ds(b * at, at)] = o
        fm[pl.ds(b * at, at)] = jnp.broadcast_to(m, (at, qn, head))
        fl[pl.ds(b * at, at)] = jnp.broadcast_to(l, (at, qn, head))
        return 0

    lax.fori_loop(0, rows // at, fresh_part, 0)

    both = ZH * qn
    shape = (both, ys * piece)
    a_row = lax.broadcasted_iota(jnp.int32, shape, 0)
    a_col = lax.broadcasted_iota(jnp.int32, shape, 1)
    token = ((a_col // piece) * ZH + zh) * tok + a_col % tok
    token = jnp.where((a_col % piece) // tok == a_row // qn, token, 1 << 20)
    lane = lax.broadcasted_iota(jnp.int32, (both, 2 * qn), 1)
    diag = lax.broadcasted_iota(jnp.int32, (both, 2 * qn), 0) % qn
    on_m, on_l = lane == diag, lane == diag + qn

    def o_copy(peer, h):
        return pltpu.make_async_remote_copy(
            src_ref=osend.at[peer, h], dst_ref=orecv.at[g, zh], send_sem=o_send_sem,
            recv_sem=o_recv_sem.at[g], device_id=(peer, y * ZH + h), device_id_type=MESH)

    def s_copy(peer, h):
        return pltpu.make_async_remote_copy(
            src_ref=ssend.at[peer, h], dst_ref=srecv.at[g, zh], send_sem=s_send_sem,
            recv_sem=s_recv_sem.at[g], device_id=(peer, y * ZH + h), device_id_type=MESH)

    def attend(i):
        src = source(i)
        pltpu.make_async_copy(qbuf.at[src], qbuf.at[src], q_recv_sem.at[src]).wait()
        q = qbuf[src].reshape(both, head)
        kv = kvrecv[i].reshape(ys * piece, 2 * head)
        s = lax.dot_general(q, kv[:, :head], (((1,), (1,)), ((), ())), preferred_element_type=jnp.float32) * scale
        keep = token < where_ref[1, src]
        s = jnp.where(keep, s, NONE)
        m = jnp.max(s, axis=1, keepdims=True)
        p = jnp.where(keep, jnp.exp(s - m), 0.0)
        l = jnp.sum(p, axis=1, keepdims=True)
        o = jnp.dot(p.astype(jnp.bfloat16), kv[:, head:], preferred_element_type=jnp.float32)
        osend[src] = o.astype(jnp.bfloat16).reshape(ZH, qn, head)
        stat = jnp.where(on_m, m, jnp.where(on_l, l, 0.0))
        ssend[src] = jnp.sum(stat.reshape(ZH, qn, 2 * qn), axis=1, keepdims=True)
        return src

    def attend_send(i, _):
        src = attend(i)
        for h in range(ZH):
            half = (zh + 1 + h) % ZH
            s_copy(src, half).start()
            o_copy(src, half).start()
        return 0

    arrived = 0
    for c in range(CHUNKS):
        while arrived < min(c + 1 + BEHIND, CHUNKS):
            for k in range(1, ys):
                kv_copy(k, arrived).wait_recv()
            arrived += 1
        lax.fori_loop(c * per, min((c + 1) * per, last), attend_send, 0)
    attend(last)
    s_copy(g, 1 - zh).start()
    o_copy(g, 1 - zh).start()
    pltpu.make_async_copy(osend.at[g, zh], orecv.at[g, zh], o_recv_sem.at[g]).start()
    pltpu.make_async_copy(ssend.at[g, zh], srecv.at[g, zh], s_recv_sem.at[g]).start()

    c_lane = lax.broadcasted_iota(jnp.int32, (qn, 2 * qn), 1)
    c_row = lax.broadcasted_iota(jnp.int32, (qn, 2 * qn), 0)

    def combine(i, _):
        src = towards(i)
        pltpu.make_async_copy(srecv.at[src], srecv.at[src], s_recv_sem.at[src]).wait()
        pltpu.make_async_copy(orecv.at[src], orecv.at[src], o_recv_sem.at[src]).wait()
        m, l, o = [fm[src]], [fl[src]], [fo[src]]
        for h in range(ZH):
            stat = jnp.broadcast_to(srecv[src, h], (qn, 2 * qn))
            m.append(jnp.sum(jnp.where(c_lane == c_row, stat, 0.0), axis=1, keepdims=True))
            l.append(jnp.sum(jnp.where(c_lane == c_row + qn, stat, 0.0), axis=1, keepdims=True))
            o.append(orecv[src, h].astype(jnp.float32))
        top = functools.reduce(jnp.maximum, m)
        w = [jnp.exp(a - top) for a in m]
        den = sum(a * b for a, b in zip(w, l))
        num = sum(a * b for a, b in zip(w, o))
        out_ref[src] = (num / den).astype(jnp.bfloat16)
        return 0

    lax.fori_loop(0, groups, combine, 0)

    for c in range(CHUNKS):
        for k in range(1, ys):
            kv_copy(k, c).wait_send()
    for ref, sem in ((qbuf, q_send_sem), (osend, o_send_sem), (ssend, s_send_sem)):
        pltpu.make_async_copy(ref.at[pl.ds(0, last)], ref.at[pl.ds(0, last)], sem).wait()
        pltpu.make_async_copy(ref.at[last, 0], ref.at[last, 0], sem).wait()


def shards(cache_blocks, prompt_len, dest_perm, new_q, new_kv):
    groups = lax.axis_size("group")
    tensors = lax.axis_size("tensor")
    requests, _, tok, heads, width = cache_blocks.shape
    head = width // 2
    slots, steps, q_here = new_q.shape[1:4]
    qn = steps * q_here
    cache = cache_blocks.reshape(requests, tok * heads, width)
    queries = new_q.reshape(slots, qn, head)
    fresh = new_kv.reshape(slots, steps, width)
    ys = tensors // ZH
    piece = ZH * tok
    bf16, f32, i32 = jnp.bfloat16, jnp.float32, jnp.int32
    hbm = pl.BlockSpec(memory_space=pltpu.HBM)
    dma = pltpu.SemaphoreType.DMA
    out = pl.pallas_call(
        functools.partial(kernel, groups, tensors),
        out_shape=jax.ShapeDtypeStruct((slots, qn, head), bf16),
        in_specs=[hbm] * 5,
        out_specs=pl.BlockSpec(memory_space=pltpu.VMEM),
        scratch_shapes=[
            pltpu.VMEM((requests, tok * heads, width), bf16),
            pltpu.VMEM((slots, qn, head), bf16),
            pltpu.VMEM((slots, steps, width), bf16),
            pltpu.VMEM(dest_perm.shape, i32),
            pltpu.VMEM(prompt_len.shape, i32),
            pltpu.VMEM((8, 128), i32),
            pltpu.SMEM((8, 128), i32),
            pltpu.VMEM((ys - 1, requests, piece, width), bf16),
            pltpu.VMEM((requests, ys, piece, width), bf16),
            pltpu.VMEM((groups, ZH, qn, head), bf16),
            pltpu.VMEM((groups, ZH, qn, head), bf16),
            pltpu.VMEM((groups, ZH, qn, head), bf16),
            pltpu.VMEM((groups, ZH, 1, 2 * qn), f32),
            pltpu.VMEM((groups, ZH, 1, 2 * qn), f32),
            pltpu.VMEM((slots, qn, head), f32),
            pltpu.VMEM((slots, qn, head), f32),
            pltpu.VMEM((slots, qn, head), f32),
            dma((CHUNKS,)),
            dma((4,)),
            pltpu.SemaphoreType.REGULAR,
            dma((ys - 1, CHUNKS)),
            dma((ys - 1, CHUNKS)),
            dma,
            dma((groups,)),
            dma,
            dma((groups,)),
            dma,
            dma((groups,)),
        ],
        compiler_params=pltpu.CompilerParams(
            collective_id=0, has_side_effects=True, vmem_limit_bytes=48 << 20),
        cost_estimate=pl.CostEstimate(flops=1 << 30, bytes_accessed=12 << 20, transcendentals=1 << 20),
    )(*(pltpu.with_memory_space_constraint(a, pltpu.HBM) for a in (cache, dest_perm, prompt_len, queries, fresh)))
    return out.reshape(1, slots, steps, q_here, head)


def solution(mesh):
    placed = (
        P("group", None, "tensor", None, None),
        P(),
        P(),
        P("group", None, None, "tensor", None),
        P("group", None, None, "tensor", None),
    )
    return jax.shard_map(
        shards,
        mesh=mesh,
        in_specs=placed,
        out_specs=P("group", None, None, "tensor", None),
        check_vma=False,
    )
```
